32 devices in a mesh: section: 2 (over y), shard: 4 (over z), rep: 4 (over x, core).
Axes of the slice: x: 2, y: 2, z: 4, core: 2. Of those that a mesh axis runs over, the one named last changes fastest.
Arguments:
- boundary: bfloat16 [2, 4096, 2048], P('section', ('shard', 'rep')), may hold values from -6 to 6
- lengths: int32 [32, 4], P(('shard', 'rep')), may hold values from 1 to 64, 128 in all within a row
- deal_order: int32 [32], P(('shard', 'rep')), may hold values from 0 to 31, as said below
- w_query: bfloat16 [2, 2048, 2048], P('section', 'shard'), may hold values from -0.125 to 0.125
- w_forget: bfloat16 [2, 2048, 2048], P('section', 'shard'), may hold values from -0.125 to 0.125
- w_input: bfloat16 [2, 2048, 2048], P('section', 'shard'), may hold values from -0.125 to 0.125
- w_out: bfloat16 [2, 2048, 2048], P('section', 'shard'), may hold values from -0.125 to 0.125
- w_gate: bfloat16 [2, 2048, 5632], P('section', 'shard'), may hold values from -0.125 to 0.125
- w_up: bfloat16 [2, 2048, 5632], P('section', 'shard'), may hold values from -0.125 to 0.125
- w_down: bfloat16 [2, 5632, 2048], P('section', 'shard'), may hold values from -0.078125 to 0.078125
- norm_mix: bfloat16 [2, 2048], P('section', 'shard'), may hold values from 0.5 to 1.5
- norm_head: bfloat16 [2, 2048], P('section', 'shard'), may hold values from 0.5 to 1.5
- norm_ffn: bfloat16 [2, 2048], P('section', 'shard'), may hold values from 0.5 to 1.5
- gate_gap: bfloat16 [2, 2048], P('section', 'shard'), may hold values from 0.0099487305 to 0.29882812
Outputs:
- boundary_out: bfloat16 [2, 4096, 2048], P('section', ('shard', 'rep'))
- grad_query: float32 [2, 2048, 2048], P('section', 'shard')
- grad_forget: float32 [2, 2048, 2048], P('section', 'shard')
- grad_input: float32 [2, 2048, 2048], P('section', 'shard')
- grad_out: float32 [2, 2048, 2048], P('section', 'shard')
- grad_gate: float32 [2, 2048, 5632], P('section', 'shard')
- grad_up: float32 [2, 2048, 5632], P('section', 'shard')
- grad_down: float32 [2, 5632, 2048], P('section', 'shard')
- mixer_norm_gradient: float32 [2, 2048], P('section', 'shard')
- grad_norm_head: float32 [2, 2048], P('section', 'shard')
- grad_norm_ffn: float32 [2, 2048], P('section', 'shard')
- grad_gate_gap: float32 [2, 2048], P('section', 'shard')
The draws below stay inside these ranges and needn't reach their ends.
Inputs may be any that keep to these rules, and one draw needn't show every extreme that they name: `lengths`: each row's entries sum to 128; the last entry is the padding at the row's end; in each row some entry equals 64. `deal_order`: each aligned block of 8 entries is a permutation of that block's own row numbers.
All inputs are finite; a program needn't handle non-finite values.
Results may differ from the reference program's by a relative error of at most 0.024.
Values may be sent and summed in bfloat16 or wider, within the bound.
No kernel may reach another device: no remote copies, remote signals or barrier semaphores. Data moves between devices by JAX's collectives and lax.ppermute only.
A program may use at most 576 MiB of HBM per device.

```python
import math
import jax
import jax.numpy as jnp
import numpy as np
from jax import lax

D = 2048
HEADS = 16
HEAD = 128
FF = 5632
LEN = 128
MICRO = 2
NSEG = 4
MAXLEN = 64
TOKENS = 4096
ROWS = 32
N_REP = 4


def draw_deal_order(key, part):
    block_rows = MICRO * N_REP
    blocks = ROWS // block_rows
    subkeys = jax.random.split(key, blocks)
    shuffled = jax.vmap(lambda subkey: jax.random.permutation(subkey, block_rows))(subkeys)
    offsets = (jnp.arange(blocks, dtype=jnp.int32) * block_rows)[:, None]
    return (shuffled.astype(jnp.int32) + offsets).reshape(ROWS)


def level_of(rng, dims, pieces, smallest, top_value):
    loudness = 1.0
    for axis_at, parts in pieces:
        draws = jax.random.uniform(jax.random.fold_in(jax.random.fold_in(rng, 6), axis_at), (parts,), jnp.float32, smallest / len(pieces), top_value / len(pieces))
        loudness = loudness * jnp.repeat(jnp.exp(draws), dims[axis_at] // parts).reshape((-1,) + (1,) * (len(dims) - 1 - axis_at))
    return loudness


def profile(count, total, limit, skew):
    portions = [(1 << 20) // math.isqrt(rank ** skew) + 1 for rank in range(2, count + 1)]
    surplus, counts = total - limit - (count - 1), [1] * (count - 1)
    while surplus > 0:
        movable = [i for i in range(count - 1) if counts[i] < limit]
        whole, remaining = sum([portions[i] for i in movable]), surplus
        for i in movable:
            more = min(limit - counts[i], max(1, remaining * portions[i] // whole), surplus)
            counts[i] = counts[i] + more
            surplus = surplus - more
    return np.array([limit] + counts)


def ragged(key, count, total, reach, slope):
    if count == 2:
        one = jax.random.randint(key, (), max(1, total - reach), min(reach, total - 1) + 1)
        return jnp.stack([one, total - one])
    sizes = jnp.asarray(profile(count, total, reach, slope), jnp.int32)
    pairs = (count - 1) // 2
    source_of, sink = sizes[1:1 + 2 * pairs:2], sizes[2:2 + 2 * pairs:2]
    margin = jnp.minimum(source_of - 1, reach - sink)
    shifted = jax.random.randint(jax.random.fold_in(key, 1), (pairs,), 0, 1 << 20) % (margin + 1)
    sizes = sizes.at[1:1 + 2 * pairs:2].set(source_of - shifted).at[2:2 + 2 * pairs:2].set(sink + shifted)
    return sizes[jax.random.permutation(jax.random.fold_in(key, 2), count)]


def normal_values(key, shape, scale, most, shards=(), kind=jnp.bfloat16):
    level = level_of(key, shape, shards, -0.22, 0.18) if shards else 1.0
    result = jax.random.normal(key, shape, jnp.float32) * scale * level
    return jnp.minimum(jnp.maximum(result, -most), most).astype(kind)


def setup_inputs(seed: int = 0) -> dict:
    splits = jax.random.split(jax.random.key(seed), 15)
    boundary = normal_values(splits[0], (2, TOKENS, D), 1.0, 6.0, ((0, 2), (1, 16)))
    lengths = jax.vmap(lambda own: ragged(own, NSEG, LEN, MAXLEN, 2))(jax.random.split(splits[1], ROWS)).reshape((ROWS, NSEG)).astype(jnp.int32)
    deal_order = draw_deal_order(jax.random.fold_in(splits[14], 71), 0)
    w_query = normal_values(splits[3], (2, D, D), D ** -0.5, 0.125, ((0, 2), (1, 4)))
    w_forget = normal_values(splits[4], (2, D, D), D ** -0.5, 0.125, ((0, 2), (1, 4)))
    w_input = normal_values(splits[5], (2, D, D), D ** -0.5, 0.125, ((0, 2), (1, 4)))
    w_out = normal_values(splits[6], (2, D, D), D ** -0.5, 0.125, ((0, 2), (1, 4)))
    w_gate = normal_values(splits[7], (2, D, FF), D ** -0.5, 0.125, ((0, 2), (1, 4)))
    w_up = normal_values(splits[8], (2, D, FF), D ** -0.5, 0.125, ((0, 2), (1, 4)))
    w_down = normal_values(splits[9], (2, FF, D), FF ** -0.5, 0.078125, ((0, 2), (1, 4)))
    norm_mix = jnp.clip(1.0 + 0.1 * jax.random.normal(splits[10], (2, D), jnp.float32), 0.5, 1.5).astype(jnp.bfloat16)
    norm_head = jnp.clip(1.0 + 0.1 * jax.random.normal(splits[11], (2, D), jnp.float32), 0.5, 1.5).astype(jnp.bfloat16)
    norm_ffn = jnp.clip(1.0 + 0.1 * jax.random.normal(splits[12], (2, D), jnp.float32), 0.5, 1.5).astype(jnp.bfloat16)
    gate_gap = jnp.clip(jnp.exp(math.log(0.29882812) - 3.4024236 * jax.random.uniform(splits[13], (2, D), jnp.float32) ** level_of(splits[13], (2, D), ((0, 2), (1, 4)), -0.2, 0.2)), 0.0099487305, 0.29882812).astype(jnp.bfloat16)
    return {"boundary": boundary, "lengths": lengths, "deal_order": deal_order, "w_query": w_query, "w_forget": w_forget, "w_input": w_input, "w_out": w_out, "w_gate": w_gate, "w_up": w_up, "w_down": w_down, "norm_mix": norm_mix, "norm_head": norm_head, "norm_ffn": norm_ffn, "gate_gap": gate_gap}


@jax.custom_vjp
def low(v):
    return lax.optimization_barrier(v.astype(jnp.bfloat16)).astype(jnp.float32)

@jax.custom_vjp
def low_back(v):
    return v

def low_keep(v):
    return (low(v), None)

def low_pass(kept, grad):
    return (grad,)

def back_keep(v):
    return (v, None)

def back_low(kept, grad):
    return (low(grad),)
low.defvjp(low_keep, low_pass)
low_back.defvjp(back_keep, back_low)
EPS = 1e-06
HEAD_EPS = 0.1
TOP_PRECISION = lax.Precision.HIGHEST

def rms_norm(value, gain):
    return value * lax.rsqrt(lax.optimization_barrier(jnp.mean(value * value, axis=-1, keepdims=True)) + EPS) * gain

def head_norm(value, gain):
    return value * lax.rsqrt(lax.optimization_barrier(jnp.mean(value * value, axis=-1, keepdims=True)) + HEAD_EPS) * gain

def matmul_high(left, right):
    return jnp.dot(left, right, precision=TOP_PRECISION)

def segment_info(lens_row):
    lens_int = lens_row.astype(jnp.int32)
    seg_ends = jnp.cumsum(lens_int).astype(jnp.int32)
    position = jnp.arange(LEN).astype(jnp.int32)
    segment_ids = lax.optimization_barrier(jnp.sum((position[:, None] >= seg_ends[None, :]).astype(jnp.int32), axis=1)).astype(jnp.int32)
    valid_mask = (position < (LEN - lens_int[-1]).astype(jnp.int32)).astype(jnp.float32)
    return (segment_ids, valid_mask)

def recur_row(row_items):
    query, keys, gates, values, segment_ids = row_items
    changes = (segment_ids[1:] != segment_ids[:-1]).astype(query.dtype)
    resets = jnp.concatenate([jnp.ones((1,), query.dtype), changes])

    def advance(relayed_state, token):
        query_vector, k, g, v, reset = token
        relayed_state = (g * (1.0 - reset))[:, :, None] * relayed_state + k[:, :, None] * v[:, None, :]
        return (relayed_state, jnp.einsum('zw,zwx->zx', query_vector, relayed_state, precision=TOP_PRECISION))
    start_state = jnp.zeros((HEADS, HEAD, HEAD), query.dtype)
    _, outputs = lax.scan(advance, start_state, (query, keys, gates, values, resets))
    return outputs

def to_heads(value):
    return value.reshape(value.shape[0], LEN, HEADS, HEAD)

def block_forward_pass(x, params, segment_ids, valid_mask):
    weight_query, weight_forget, weight_input, weight_out, weight_gate, weight_up, weight_down, gain_mix, gain_head, gain_ffn, gap = params
    normed_in = low(rms_norm(x, gain_mix))
    query_vector = low_back(matmul_high(normed_in, weight_query))
    f = low_back(matmul_high(normed_in, weight_forget))
    v = low_back(matmul_high(normed_in, weight_input))
    closed = jax.nn.sigmoid(-f) * gap
    k = closed * valid_mask[..., None]
    g = 1.0 - closed
    o = lax.map(jax.checkpoint(recur_row), (to_heads(query_vector), to_heads(k), to_heads(g), to_heads(v), segment_ids))
    mixed = low(head_norm(o, gain_head.reshape(HEADS, HEAD)).reshape(x.shape))
    resid_mid = x + low_back(matmul_high(mixed, weight_out))
    normed_mid = low(rms_norm(resid_mid, gain_ffn))
    gate_value = low_back(matmul_high(normed_mid, weight_gate))
    up_value = low_back(matmul_high(normed_mid, weight_up))
    hidden = low(jax.nn.silu(gate_value) * up_value)
    return (resid_mid + low_back(matmul_high(hidden, weight_down))) * valid_mask[..., None]

def reference(boundary, lengths, deal_order, w_query, w_forget, w_input, w_out, w_gate, w_up, w_down, norm_mix, norm_head, norm_ffn, gate_gap):
    order_index = deal_order.astype(jnp.int32)
    dealt = boundary[0].astype(jnp.float32).reshape(ROWS, LEN, D)[order_index]
    cotangent = boundary[1].astype(jnp.float32).reshape(ROWS, LEN, D)
    dealt_lengths = lengths.astype(jnp.int32)[order_index]
    segment_ids, valid_mask = jax.vmap(segment_info)(dealt_lengths)
    valid_mask = valid_mask.astype(dealt.dtype)
    params = tuple((weight.astype(jnp.float32) for weight in (w_query, w_forget, w_input, w_out, w_gate, w_up, w_down, norm_mix, norm_head, norm_ffn, gate_gap)))

    def forward(inputs, all_params):
        first_params = tuple((weight[0] for weight in all_params))
        second_params = tuple((weight[1] for weight in all_params))
        first = low(low_back(block_forward_pass(inputs, first_params, segment_ids, valid_mask)))
        return block_forward_pass(first, second_params, segment_ids, valid_mask)
    second, pullback = jax.vjp(forward, dealt, params)
    grad_dealt, grads = pullback(cotangent)
    inverse_order = jnp.argsort(order_index).astype(jnp.int32)
    result_values = grad_dealt[inverse_order]
    boundary_out = jnp.stack([result_values.reshape(TOKENS, D), second.reshape(TOKENS, D)]).astype(jnp.bfloat16)
    return (boundary_out, grads[0], grads[1], grads[2], grads[3], grads[4], grads[5], grads[6], grads[7], grads[8], grads[9], grads[10])
```

```python
import jax
import jax.numpy as jnp
from jax import lax
from jax.sharding import PartitionSpec as P

HEADS = 16
EPS = 1e-06
HEAD_EPS = 0.1
TOP_PRECISION = lax.Precision.HIGHEST
BF16 = jnp.bfloat16
F32 = jnp.float32


def swap(block, stage):
    axis, distance = stage
    return lax.ppermute(block, axis, [(i, i ^ distance) for i in range(lax.axis_size(axis))])


def one_way(block, source):
    return lax.ppermute(block, "section", [(source, 1 - source)])


def spread(block, stages):
    for stage in stages:
        block = jnp.concatenate([block, swap(block, stage)], axis=0)
    return block


def collapse(send, keep, stages):
    for stage in stages[::-1]:
        total = keep + swap(send.astype(BF16), stage).astype(F32)
        half = total.shape[0] // 2
        keep, send = total[:half], total[half:]
    return total


def reduced_product(left, right, stages):
    half = left.shape[0] // 2
    return collapse(product(left[half:], right), product(left[:half], right), stages)


def product(left, right):
    return jnp.dot(left, right, preferred_element_type=F32)


def product_t(left, right):
    return lax.dot_general(left, right, (((1,), (1,)), ((), ())), preferred_element_type=F32)


def weight_term(act_rows, grad_rows):
    return lax.dot_general(
        act_rows, grad_rows, (((0,), (0,)), ((), ())), preferred_element_type=F32
    ).astype(BF16)


def rms_norm(value, gain):
    return value * lax.rsqrt(jnp.mean(value * value, axis=-1, keepdims=True) + EPS) * gain


def head_norm(value, gain):
    return value * lax.rsqrt(jnp.mean(value * value, axis=-1, keepdims=True) + HEAD_EPS) * gain


def segment_info(lens_row, length):
    seg_ends = jnp.cumsum(lens_row)
    position = jnp.arange(length)
    segment_ids = jnp.sum((position[:, None] >= seg_ends[None, :]).astype(jnp.int32), axis=1)
    valid_mask = (position < length - lens_row[-1]).astype(F32)
    return (segment_ids, valid_mask)


def mixer(q, f, v, gap, gain_head, valid_mask, same):
    closed = jax.nn.sigmoid(-f) * gap
    k = closed * valid_mask[:, :, None, None]
    decay = jnp.cumsum(jnp.log(1.0 - closed), axis=1)
    query_decayed = q * jnp.exp(decay)
    key_decayed = k * jnp.exp(-decay)
    scores = (
        jnp.einsum("rthk,rshk->rhts", query_decayed, key_decayed, precision=TOP_PRECISION)
        * same[:, None]
    )
    o = jnp.einsum("rhts,rshv->rthv", scores, v, precision=TOP_PRECISION)
    return head_norm(o, gain_head)


def split_weights(
    w_query, w_forget, w_input, w_out, w_gate, w_up, w_down, ident, shards, group, sharing
):
    model_width = w_query.shape[1]
    head = model_width // HEADS
    per_device = HEADS // group
    per_shard = HEADS // shards
    cluster, member = ident // sharing, ident % sharing
    each = sharing * per_device // shards

    def head_columns(weight):
        parts = []
        for t in range(per_device):
            at = member * per_device + t
            number = per_shard * (at // each) + cluster * each + at % each
            parts.append(lax.dynamic_slice_in_dim(weight, number * head, head, 1))
        return parts

    qfv = jnp.concatenate(
        head_columns(w_query) + head_columns(w_forget) + head_columns(w_input), axis=1
    )
    width = model_width // sharing
    out = lax.dynamic_slice(
        w_out, (cluster * each * head, member * width), (each * head, width)
    )
    local_ff = w_down.shape[0]
    own_ff = local_ff // group

    def ff_columns(weight):
        return [
            lax.dynamic_slice_in_dim(weight, local_ff * s + own_ff * ident, own_ff, 1)
            for s in range(shards)
        ]

    gate_up = jnp.concatenate(ff_columns(w_gate) + ff_columns(w_up), axis=1)
    down = lax.dynamic_slice_in_dim(w_down, own_ff * ident, own_ff, 0)
    return (qfv, out, gate_up, down)


def local(
    boundary,
    lengths,
    deal_order,
    w_query,
    w_forget,
    w_input,
    w_out,
    w_gate,
    w_up,
    w_down,
    norm_mix,
    norm_head,
    norm_ffn,
    gate_gap,
):
    micro = deal_order.shape[0]
    reps = lax.axis_size("rep")
    shards = lax.axis_size("shard")
    group = 2 * reps
    model_width = boundary.shape[2]
    length = boundary.shape[1] // micro
    head = model_width // HEADS
    per_device = HEADS // group
    per_shard = HEADS // shards
    sharing = shards * group // HEADS
    each = sharing * per_device // shards
    section = lax.axis_index("section")
    rep = lax.axis_index("rep")
    shard = lax.axis_index("shard")
    on_first = section == 0
    ident = section * reps + rep

    rep_stages = []
    distance = reps // 2
    while distance:
        rep_stages.append(("rep", distance))
        distance //= 2
    stages = [("section", 1)] + rep_stages
    share_stages = [stage for stage in rep_stages if stage[1] < sharing]

    def codes(some):
        order = [0]
        for axis, distance in some:
            bit = reps if axis == "section" else distance
            order = order + [o ^ bit for o in order]
        return order

    def places(some):
        order = codes(some)
        slot = [0] * len(order)
        for at, code in enumerate(order):
            slot[code] = at
        return jnp.array(slot, jnp.int32)

    plane_order = jnp.array(codes(stages), jnp.int32)
    plane_place = places(stages)
    rep_place = places(rep_stages)

    block_rows = micro * reps
    numbers = lax.all_gather(
        jnp.concatenate([deal_order[:, None], lengths], axis=1), "rep", axis=0, tiled=True
    )
    block_order = numbers[:, 0] % block_rows
    block_lengths = numbers[:, 1:]
    gains = jnp.stack([norm_mix[0], norm_ffn[0], norm_head[0], gate_gap[0]])
    gains = lax.all_gather(gains, ("section", "shard"), axis=0, tiled=False)
    gains = gains.reshape(2, shards, 4, -1).transpose(0, 2, 1, 3).reshape(2, 4, model_width)
    gains = gains.astype(F32)

    local_weights = (w_query[0], w_forget[0], w_input[0], w_out[0], w_gate[0], w_up[0], w_down[0])
    kept = split_weights(*local_weights, ident, shards, group, sharing)
    sent = split_weights(
        *local_weights, (1 - section) * reps + rep, shards, group, sharing
    )
    received = [swap(piece, ("section", 1)) for piece in sent]
    layer_pieces = (
        [jnp.where(on_first, a, b) for a, b in zip(kept, received)],
        [jnp.where(on_first, b, a) for a, b in zip(kept, received)],
    )
    layer_weights = []
    member = ident % sharing
    for layer in range(2):
        qfv, out, gate_up, down = [
            lax.all_gather(piece, "shard", axis=0, tiled=True) for piece in layer_pieces[layer]
        ]
        wide = spread(out[None], share_stages)
        wide = wide[places(share_stages)[jnp.arange(sharing) ^ member]]
        wide = jnp.swapaxes(wide, 0, 1).reshape(shards * each * head, model_width)
        out = lax.dynamic_slice_in_dim(wide, member * per_device * head, per_device * head, 0)
        layer_weights.append((qfv, out, gate_up, down))

    cluster = ident // sharing
    own_heads = []
    for t in range(per_device):
        at = member * per_device + t
        own_heads.append(per_shard * (at // each) + cluster * each + at % each)

    def own_channels(vector):
        return jnp.stack(
            [lax.dynamic_slice_in_dim(vector, number * head, head, 0) for number in own_heads]
        )

    holder = plane_order ^ ident
    dealt_row = (holder % reps) * micro + holder // reps
    arrival_row = block_order[dealt_row]
    segment_ids, valid_mask = jax.vmap(lambda lens_row: segment_info(lens_row, length))(
        block_lengths[arrival_row]
    )
    causal = jnp.tril(jnp.ones((length, length), F32))
    same = (segment_ids[:, :, None] == segment_ids[:, None, :]).astype(F32) * causal
    valid_own = valid_mask[0][:, None]

    rows = boundary[0].reshape(micro, length, model_width)
    first_rows = jnp.where(on_first, rows, one_way(rows, 0))
    arrivals = spread(first_rows, rep_stages)
    slot = rep_place[(arrival_row // micro) ^ rep] * micro + arrival_row % micro
    dealt = arrivals[slot]
    own_cotangent = jnp.where(on_first, one_way(rows[0], 1), rows[1]).astype(F32)

    def forward(x_own, normed_all, weights, gain):
        qfv_weight, out_weight, gate_up_weight, down_weight = weights
        qfv = product(normed_all, qfv_weight).reshape(group, length, 3, per_device, head)
        mixed, pull_mix = jax.vjp(
            lambda a, b, c, d, e: mixer(a, b, c, d, e, valid_mask, same),
            qfv[:, :, 0],
            qfv[:, :, 1],
            qfv[:, :, 2],
            own_channels(gain[3]),
            own_channels(gain[2]),
        )
        mixed = mixed.reshape(group * length, per_device * head).astype(BF16)
        resid_mid = x_own + reduced_product(mixed, out_weight, stages)
        mid_value, pull_mid = jax.vjp(rms_norm, resid_mid, gain[1])
        normed_mid = spread(mid_value.astype(BF16), stages)
        gate_up = product(normed_mid, gate_up_weight)
        half = gate_up.shape[1] // 2
        hidden, pull_act = jax.vjp(
            lambda a, b: jax.nn.silu(a) * b, gate_up[:, :half], gate_up[:, half:]
        )
        hidden = hidden.astype(BF16)
        result = (resid_mid + reduced_product(hidden, down_weight, stages)) * valid_own
        return result.astype(BF16), (normed_all, mixed, normed_mid, hidden, pull_mix, pull_mid, pull_act)

    def transposed_sum(left, right, stages):
        half = left.shape[0] // 2
        return collapse(product_t(left[half:], right), product_t(left[:half], right), stages)

    def backward(grad_out, weights, kept_state, pull_in):
        qfv_weight, out_weight, gate_up_weight, down_weight = weights
        normed_all, mixed, normed_mid, hidden, pull_mix, pull_mid, pull_act = kept_state
        d_out = grad_out * valid_own
        d_down = spread(d_out.astype(BF16), stages)
        d_hidden = product_t(d_down, down_weight)
        d_gate_up = jnp.concatenate(pull_act(d_hidden), axis=1).astype(BF16)
        term_down = weight_term(hidden, d_down)
        term_gate_up = weight_term(normed_mid, d_gate_up)
        more, grad_ffn = pull_mid(transposed_sum(d_gate_up, gate_up_weight, stages))
        d_resid = d_out + more
        d_attn = spread(d_resid.astype(BF16), stages)
        d_mixed = product_t(d_attn, out_weight).reshape(group, length, per_device, head)
        d_q, d_f, d_v, grad_gap, grad_head = pull_mix(d_mixed)
        d_qfv = jnp.stack([d_q, d_f, d_v], axis=2).astype(BF16)
        d_qfv = d_qfv.reshape(group * length, 3 * per_device * head)
        term_out = weight_term(mixed, d_attn)
        term_qfv = weight_term(normed_all, d_qfv)
        more, grad_mix = pull_in(transposed_sum(d_qfv, qfv_weight, stages))
        d_x = d_resid + more
        wide = spread(term_out[None], share_stages)
        wide = wide[places(share_stages)[jnp.arange(sharing) ^ member]]
        wide = wide.reshape(sharing * per_device * head, model_width)
        term_out = lax.dynamic_slice_in_dim(
            wide, member * (model_width // sharing), model_width // sharing, 1
        )
        small = jnp.zeros((4, model_width), F32).at[0].set(grad_mix).at[1].set(grad_ffn)
        for t in range(per_device):
            column = own_heads[t] * head
            small = lax.dynamic_update_slice(small, grad_head[t][None], (2, column))
            small = lax.dynamic_update_slice(small, grad_gap[t][None], (3, column))
        return d_x, (term_qfv, term_out, term_gate_up, term_down), small

    dealt_f32 = dealt.astype(F32)
    normed_first = rms_norm(dealt_f32, gains[0, 0]).astype(BF16)
    _, pull_in_first = jax.vjp(rms_norm, dealt_f32[0], gains[0, 0])
    first, kept_first = forward(
        dealt_f32[0],
        normed_first.reshape(group * length, model_width),
        layer_weights[0],
        gains[0],
    )
    first_f32 = first.astype(F32)
    normed_second, pull_in_second = jax.vjp(rms_norm, first_f32, gains[1, 0])
    second, kept_second = forward(
        first_f32, spread(normed_second.astype(BF16), stages), layer_weights[1], gains[1]
    )
    d_first, terms_second, small_second = backward(
        own_cotangent, layer_weights[1], kept_second, pull_in_second
    )
    d_dealt, terms_first, small_first = backward(
        d_first.astype(BF16).astype(F32), layer_weights[0], kept_first, pull_in_first
    )

    all_grads = spread(d_dealt.astype(BF16)[None], stages)
    inverse = jnp.argsort(block_order)
    own_dealt = lax.dynamic_slice_in_dim(inverse, rep * micro, micro, 0)
    own_holder = (own_dealt % micro) * reps + own_dealt // micro
    back_rows = all_grads[plane_place[own_holder ^ ident]]
    second_rows = jnp.stack([one_way(second, 0), second])
    boundary_out = jnp.where(on_first, back_rows, second_rows).reshape(
        1, micro * length, model_width
    )

    absolute = plane_place[jnp.arange(group) ^ ident]
    pieces = []
    for number in range(4):
        summed = [
            lax.psum_scatter(terms[number], "shard", scatter_dimension=0, tiled=True)
            for terms in (terms_first, terms_second)
        ]
        keep = jnp.where(on_first, summed[0], summed[1])[None]
        send = jnp.where(on_first, summed[1], summed[0])[None]
        pair = jnp.concatenate([keep, swap(send, ("section", 1))], axis=0)
        pieces.append(spread(pair, rep_stages)[absolute].astype(F32))
    qfv, out, gate_up, down = pieces
    local_rows = qfv.shape[1]
    clusters = group // sharing
    qfv = qfv.reshape(clusters, sharing, local_rows, 3, per_device, head)
    qfv = qfv.transpose(3, 2, 1, 4, 0, 5).reshape(
        3, local_rows, shards, each, clusters, head
    )
    qfv = qfv.transpose(0, 1, 2, 4, 3, 5).reshape(3, local_rows, model_width)
    out = out.reshape(clusters, sharing, each * head, model_width // sharing)
    out = out.transpose(0, 2, 1, 3).reshape(local_rows, model_width)
    own_ff = w_down.shape[1] // group
    gate_up = gate_up.reshape(group, local_rows, 2, shards, own_ff)
    gate_up = gate_up.transpose(2, 1, 3, 0, 4).reshape(2, local_rows, -1)
    down = down.reshape(-1, model_width)

    small = jnp.stack([small_first, small_second])
    for stage in stages:
        small = small + swap(small, stage)
    small = jnp.where(on_first, small[0], small[1])
    small = jnp.sum(lax.all_gather(small, "shard", axis=0, tiled=False), axis=0)
    small = lax.dynamic_slice_in_dim(small, shard * local_rows, local_rows, 1)

    return (
        boundary_out,
        qfv[0][None],
        qfv[1][None],
        qfv[2][None],
        out[None],
        gate_up[0][None],
        gate_up[1][None],
        down[None],
        small[0][None],
        small[2][None],
        small[1][None],
        small[3][None],
    )


def solution(mesh):
    row_blocks = P("section", ("shard", "rep"), None)
    weight = P("section", "shard", None)
    vector = P("section", "shard")
    return jax.shard_map(
        local,
        mesh=mesh,
        in_specs=(row_blocks, P(("shard", "rep"), None), P(("shard", "rep")))
        + (weight,) * 7
        + (vector,) * 4,
        out_specs=(row_blocks,) + (weight,) * 7 + (vector,) * 4,
        check_vma=False,
    )
```

```python
import functools

import jax
import jax.numpy as jnp
from jax import lax
from jax.experimental import pallas as pl
from jax.experimental.pallas import tpu as pltpu
from jax.sharding import PartitionSpec as P

HEADS = 16
EPS = 1e-06
HEAD_EPS = 0.1
TOP_PRECISION = lax.Precision.HIGHEST
BF16 = jnp.bfloat16
F32 = jnp.float32


def swap(block, stage):
    axis, distance = stage
    return lax.ppermute(block, axis, [(i, i ^ distance) for i in range(lax.axis_size(axis))])


def one_way(block, source):
    return lax.ppermute(block, "section", [(source, 1 - source)])


def spread(block, stages):
    for stage in stages:
        block = jnp.concatenate([block, swap(block, stage)], axis=0)
    return block


def orders(stages):
    outer = stages[:-1]
    turned = outer[1:] + outer[:1]
    codes = []
    for some in (outer, turned):
        order = [0]
        for stage in some:
            order = order + [o ^ (1 << stages.index(stage)) for o in order]
        codes.append(order)
    return outer, turned, codes[0], codes[1]


def blocks_in_order(value, source, target):
    size = value.shape[0] // len(source)
    return jnp.concatenate(
        [value[size * source.index(c) : size * (source.index(c) + 1)] for c in target], axis=0
    )


def join_kernel(order_ref, left, right, far_left, far_right, whole):
    half = left.shape[1]
    whole[0, :, :half] = left[...]
    whole[0, :, half:] = right[...]
    whole[1, :, :half] = far_left[...]
    whole[1, :, half:] = far_right[...]


def join_halves(halves, order):
    rows, half = halves[0].shape
    tile = rows // len(order)
    plain = pl.BlockSpec((tile, half), lambda i, order: (i, 0))
    turned = pl.BlockSpec((tile, half), lambda i, order: (order[i], 0))
    whole = pl.pallas_call(
        join_kernel,
        grid_spec=pltpu.PrefetchScalarGridSpec(
            num_scalar_prefetch=1,
            grid=(len(order),),
            in_specs=[plain, turned, plain, turned],
            out_specs=pl.BlockSpec((2, tile, 2 * half), lambda i, order: (0, i, 0)),
        ),
        out_shape=jax.ShapeDtypeStruct((2, rows, 2 * half), halves[0].dtype),
        compiler_params=pltpu.CompilerParams(vmem_limit_bytes=32 << 20),
    )(jnp.array(order, jnp.int32), *halves)
    return whole.reshape(2 * rows, 2 * half)


def spread_rows(block, stages, tie=None):
    outer, turned, codes, turned_codes = orders(stages)
    half = block.shape[1] // 2
    left, right = block[:, :half], block[:, half:]
    for number, (stage, other) in enumerate(zip(outer, turned)):
        left = jnp.concatenate([left, swap(left, stage)], axis=0)
        right = jnp.concatenate([right, swap(right, other)], axis=0)
        if number == len(outer) - 1 and tie is not None:
            left, right, tie = lax.optimization_barrier((left, right, tie))
    halves = (left, right, swap(left, stages[-1]), swap(right, stages[-1]))
    return join_halves(halves, [turned_codes.index(c) for c in codes]), tie


def collapse(send, keep, stages):
    outer, turned, codes, turned_codes = orders(stages)
    total = keep + swap(send.astype(BF16), stages[-1]).astype(F32)
    half = total.shape[1] // 2
    left, right = total[:, :half], blocks_in_order(total[:, half:], codes, turned_codes)
    for stage, other in zip(outer[::-1], turned[::-1]):
        size = left.shape[0] // 2
        left_in = swap(left[size:].astype(BF16), stage)
        right_in = swap(right[size:].astype(BF16), other)
        left = left[:size] + left_in.astype(F32)
        right = right[:size] + right_in.astype(F32)
    return jnp.concatenate([left, right], axis=1)


def reduced_product(left, right, stages):
    half = left.shape[0] // 2
    return collapse(product(left[half:], right), product(left[:half], right), stages)


def product(left, right):
    return jnp.dot(left, right, preferred_element_type=F32)


def product_t(left, right):
    return lax.dot_general(left, right, (((1,), (1,)), ((), ())), preferred_element_type=F32)


def weight_term(act_rows, grad_rows):
    return lax.dot_general(
        act_rows, grad_rows, (((0,), (0,)), ((), ())), preferred_element_type=F32
    ).astype(BF16)


def rms_norm(value, gain):
    return value * lax.rsqrt(jnp.mean(value * value, axis=-1, keepdims=True) + EPS) * gain


def head_norm(value, gain):
    return value * lax.rsqrt(jnp.mean(value * value, axis=-1, keepdims=True) + HEAD_EPS) * gain


def segment_info(lens_row, length):
    seg_ends = jnp.cumsum(lens_row)
    position = jnp.arange(length)
    segment_ids = jnp.sum((position[:, None] >= seg_ends[None, :]).astype(jnp.int32), axis=1)
    valid_mask = (position < length - lens_row[-1]).astype(F32)
    return (segment_ids, valid_mask)


def mixer(q, f, v, gap, gain_head, valid_mask, same):
    closed = jax.nn.sigmoid(-f) * gap
    k = closed * valid_mask[:, :, None, None]
    decay = jnp.cumsum(jnp.log(1.0 - closed), axis=1)
    query_decayed = q * jnp.exp(decay)
    key_decayed = k * jnp.exp(-decay)
    scores = (
        jnp.einsum("rthk,rshk->rhts", query_decayed, key_decayed, precision=TOP_PRECISION)
        * same[:, None]
    )
    o = jnp.einsum("rhts,rshv->rthv", scores, v, precision=TOP_PRECISION)
    return head_norm(o, gain_head)


def place_mixer_kernel(wide, columns, corners, *refs):
    sources, (query_ref, forget_ref, input_ref, out_ref) = refs[:-4], refs[-4:]
    step = pl.program_id(0)
    head = wide // (columns.shape[0] // len(sources))
    for j, source in enumerate(sources):
        for kind, target in enumerate((query_ref, forget_ref, input_ref)):
            for t in range(wide // head):
                at = pl.multiple_of(columns[j * (wide // head) + t], head)
                low = kind * wide + t * head
                target[:, pl.ds(at, head)] = source[:, low : low + head].astype(F32)
        row = pl.multiple_of(corners[2 * j], source.shape[0])
        column = pl.multiple_of(corners[2 * j + 1] + step * wide, wide)
        out_ref[pl.ds(row, source.shape[0]), pl.ds(column, wide)] = source[
            :, 3 * wide : 4 * wide
        ].astype(F32)


def place_mixer(sources, columns, corners, tile, model_width):
    rows, total = sources[0].shape
    return pl.pallas_call(
        functools.partial(place_mixer_kernel, total // 4),
        grid_spec=pltpu.PrefetchScalarGridSpec(
            num_scalar_prefetch=2,
            grid=(rows // tile,),
            in_specs=[pl.BlockSpec((tile, total), lambda i, *_: (i, 0))] * len(sources),
            out_specs=[pl.BlockSpec((tile, model_width), lambda i, *_: (i, 0))] * 3
            + [pl.BlockSpec((rows, model_width), lambda i, *_: (0, 0))],
        ),
        out_shape=[jax.ShapeDtypeStruct((rows, model_width), F32)] * 4,
        compiler_params=pltpu.CompilerParams(vmem_limit_bytes=48 << 20),
    )(columns, corners, *sources)


def place_columns_kernel(shards, ident_ref, *refs):
    sources, targets = refs[:-2], refs[-2:]
    values = [source[...] for source in sources]
    bit = 1
    while bit < len(values):
        on = (ident_ref[0] & bit) != 0
        values = [jnp.where(on, values[j ^ bit], values[j]) for j in range(len(values))]
        bit *= 2
    wide = values[0].shape[1] // (2 * shards)
    for kind, target in enumerate(targets):
        parts = []
        for s in range(shards):
            low = (kind * shards + s) * wide
            parts += [value[:, low : low + wide] for value in values]
        target[...] = jnp.concatenate(parts, axis=1).astype(F32)


def place_columns(sources, ident, shards):
    rows, total = sources[0].shape
    tile = 64
    width = len(sources) * total // 2
    return pl.pallas_call(
        functools.partial(place_columns_kernel, shards),
        grid_spec=pltpu.PrefetchScalarGridSpec(
            num_scalar_prefetch=1,
            grid=(rows // tile,),
            in_specs=[pl.BlockSpec((tile, total), lambda i, *_: (i, 0))] * len(sources),
            out_specs=[pl.BlockSpec((tile, width), lambda i, *_: (i, 0))] * 2,
        ),
        out_shape=[jax.ShapeDtypeStruct((rows, width), F32)] * 2,
        compiler_params=pltpu.CompilerParams(vmem_limit_bytes=48 << 20),
    )(ident[None], *sources)


def place_rows_kernel(ident_ref, *refs):
    sources, target = refs[:-1], refs[-1]
    for j, source in enumerate(sources):
        at = pl.multiple_of((ident_ref[0] ^ j) * source.shape[0], 8)
        target[pl.ds(at, source.shape[0]), :] = source[...].astype(F32)


def place_rows(sources, ident):
    rows, width = sources[0].shape
    tile = 512
    return pl.pallas_call(
        place_rows_kernel,
        grid_spec=pltpu.PrefetchScalarGridSpec(
            num_scalar_prefetch=1,
            grid=(width // tile,),
            in_specs=[pl.BlockSpec((rows, tile), lambda i, *_: (0, i))] * len(sources),
            out_specs=pl.BlockSpec((rows * len(sources), tile), lambda i, *_: (0, i)),
        ),
        out_shape=jax.ShapeDtypeStruct((rows * len(sources), width), F32),
        compiler_params=pltpu.CompilerParams(vmem_limit_bytes=48 << 20),
    )(ident[None], *sources)


def split_weights(
    w_query, w_forget, w_input, w_out, w_gate, w_up, w_down, ident, shards, group, sharing
):
    model_width = w_query.shape[1]
    head = model_width // HEADS
    per_device = HEADS // group
    per_shard = HEADS // shards
    cluster, member = ident // sharing, ident % sharing
    each = sharing * per_device // shards

    def head_columns(weight):
        parts = []
        for t in range(per_device):
            at = member * per_device + t
            number = per_shard * (at // each) + cluster * each + at % each
            parts.append(lax.dynamic_slice_in_dim(weight, number * head, head, 1))
        return parts

    width = model_width // sharing
    out = lax.dynamic_slice(
        w_out, (cluster * each * head, member * width), (each * head, width)
    )
    wide = per_device * head
    out = jnp.concatenate([out[:, b : b + wide] for b in range(0, width, wide)], axis=0)
    mix = jnp.concatenate(
        head_columns(w_query) + head_columns(w_forget) + head_columns(w_input) + [out], axis=1
    )
    local_ff = w_down.shape[0]
    own_ff = local_ff // group

    def ff_columns(weight):
        return [
            lax.dynamic_slice_in_dim(weight, local_ff * s + own_ff * ident, own_ff, 1)
            for s in range(shards)
        ]

    gate_up = jnp.concatenate(ff_columns(w_gate) + ff_columns(w_up), axis=1)
    down = lax.dynamic_slice_in_dim(w_down, own_ff * ident, own_ff, 0)
    return (mix, gate_up, down)


def local(
    boundary,
    lengths,
    deal_order,
    w_query,
    w_forget,
    w_input,
    w_out,
    w_gate,
    w_up,
    w_down,
    norm_mix,
    norm_head,
    norm_ffn,
    gate_gap,
):
    micro = deal_order.shape[0]
    reps = lax.axis_size("rep")
    shards = lax.axis_size("shard")
    group = 2 * reps
    model_width = boundary.shape[2]
    length = boundary.shape[1] // micro
    head = model_width // HEADS
    per_device = HEADS // group
    per_shard = HEADS // shards
    sharing = shards * group // HEADS
    each = sharing * per_device // shards
    section = lax.axis_index("section")
    rep = lax.axis_index("rep")
    shard = lax.axis_index("shard")
    on_first = section == 0
    ident = section * reps + rep

    rep_stages = []
    distance = reps // 2
    while distance:
        rep_stages.append(("rep", distance))
        distance //= 2
    stages = [("section", 1)] + rep_stages
    share_stages = [stage for stage in rep_stages if stage[1] < sharing]

    def codes(some):
        order = [0]
        for axis, distance in some:
            bit = reps if axis == "section" else distance
            order = order + [o ^ bit for o in order]
        return order

    def places(some):
        order = codes(some)
        slot = [0] * len(order)
        for at, code in enumerate(order):
            slot[code] = at
        return jnp.array(slot, jnp.int32)

    plane_order = jnp.array(codes(stages), jnp.int32)
    plane_place = places(stages)
    rep_place = places(rep_stages)

    gains = jnp.stack([norm_mix[0], norm_ffn[0], norm_head[0], gate_gap[0]])
    shard_stages = []
    distance = shards // 2
    while distance:
        shard_stages.append(("shard", distance))
        distance //= 2
    gains = spread(gains[None], shard_stages)
    gains = gains[places(shard_stages)[jnp.arange(shards) ^ shard]]
    gains = spread(gains[None], [("section", 1)])[jnp.arange(2) ^ section]

    local_weights = (w_query[0], w_forget[0], w_input[0], w_out[0], w_gate[0], w_up[0], w_down[0])
    kept = split_weights(*local_weights, ident, shards, group, sharing)
    sent = split_weights(
        *local_weights, (1 - section) * reps + rep, shards, group, sharing
    )
    received = [swap(piece, ("section", 1)) for piece in sent]
    mix_first, gate_up_first, down_first = [
        jnp.where(on_first, a, b) for a, b in zip(kept, received)
    ]
    mix_second, gate_up_second, down_second = [
        jnp.where(on_first, b, a) for a, b in zip(kept, received)
    ]

    mix_first, gains = lax.optimization_barrier((mix_first, gains))

    def over_shard(piece):
        return lax.all_gather(piece, "shard", axis=0, tiled=True)

    member = ident % sharing
    cluster = ident // sharing
    wide = per_device * head
    local_rows = model_width // shards

    def mixer_weights(mix):
        mix = over_shard(mix)
        out = mix[:, 3 * wide :].reshape(shards, -1, each * head, wide)
        out = out.transpose(0, 2, 1, 3).reshape(shards * each * head, model_width // sharing)
        out = spread(out[None], share_stages)
        out = out[places(share_stages)[jnp.arange(sharing) ^ member]]
        out = jnp.swapaxes(out, 0, 1).reshape(shards * each * head, model_width)
        out = lax.dynamic_slice_in_dim(out, member * wide, wide, 0)
        return (mix[:, : 3 * wide], out)

    block_rows = micro * reps
    numbers = jnp.concatenate([deal_order[:, None], lengths], axis=1)
    numbers = spread(numbers[None], rep_stages)[rep_place[jnp.arange(reps) ^ rep]]
    numbers = numbers.reshape(block_rows, -1)
    block_order = numbers[:, 0] % block_rows
    block_lengths = numbers[:, 1:]
    gains = gains.reshape(2, shards, 4, -1).transpose(0, 2, 1, 3).reshape(2, 4, model_width)
    gains = gains.astype(F32)

    def head_number(device, t):
        at = device % sharing * per_device + t
        return per_shard * (at // each) + device // sharing * each + at % each

    own_heads = [head_number(ident, t) for t in range(per_device)]

    def own_channels(vector):
        return jnp.stack(
            [lax.dynamic_slice_in_dim(vector, number * head, head, 0) for number in own_heads]
        )

    holder = plane_order ^ ident
    dealt_row = (holder % reps) * micro + holder // reps
    arrival_row = block_order[dealt_row]
    segment_ids, valid_mask = jax.vmap(lambda lens_row: segment_info(lens_row, length))(
        block_lengths[arrival_row]
    )
    causal = jnp.tril(jnp.ones((length, length), F32))
    same = (segment_ids[:, :, None] == segment_ids[:, None, :]).astype(F32) * causal
    valid_own = valid_mask[0][:, None]

    rows = boundary[0].reshape(micro, length, model_width)
    first_rows = jnp.where(on_first, rows, one_way(rows, 0))
    arrivals = spread(first_rows, rep_stages)
    slot = rep_place[(arrival_row // micro) ^ rep] * micro + arrival_row % micro
    dealt = arrivals[slot]
    own_cotangent = jnp.where(on_first, one_way(rows[0], 1), rows[1]).astype(F32)

    d_down_second, _ = spread_rows((own_cotangent * valid_own).astype(BF16), stages)

    def forward(x_own, normed_all, mix, gate_up_piece, gain, down_pieces=None, down_weight=None):
        qfv_weight, out_weight = mixer_weights(mix)
        qfv = product(normed_all, qfv_weight).reshape(group, length, 3, per_device, head)
        mixed, pull_mix = jax.vjp(
            lambda a, b, c, d, e: mixer(a, b, c, d, e, valid_mask, same),
            qfv[:, :, 0],
            qfv[:, :, 1],
            qfv[:, :, 2],
            own_channels(gain[3]),
            own_channels(gain[2]),
        )
        mixed = mixed.reshape(group * length, per_device * head).astype(BF16)
        if down_weight is None:
            mixed, down_pieces = lax.optimization_barrier((mixed, down_pieces))
            down_weight = over_shard(down_pieces).reshape(shards, 2, -1, model_width)
            down_weight = [down_weight[:, i].reshape(-1, model_width) for i in range(2)]
            gate_up_weight, tied = over_shard(gate_up_piece), None
        else:
            down_weight = [down_weight]
            gate_up_weight = tied = over_shard(gate_up_piece)
        resid_mid = x_own + reduced_product(mixed, out_weight, stages)
        mid_value, pull_mid = jax.vjp(rms_norm, resid_mid, gain[1])
        normed_mid, tied = spread_rows(mid_value.astype(BF16), stages, tied)
        early = ()
        if tied is not None:
            gate_up_weight = tied
            early = product_t(d_down_second, down_weight[0])
            normed_mid, early = lax.optimization_barrier((normed_mid, early))
        gate_up = product(normed_mid, gate_up_weight)
        half = gate_up.shape[1] // 2
        hidden, pull_act = jax.vjp(
            lambda a, b: jax.nn.silu(a) * b, gate_up[:, :half], gate_up[:, half:]
        )
        hidden = hidden.astype(BF16)
        if tied is None:
            hidden, early = lax.optimization_barrier((hidden, d_down_second))
        result = (resid_mid + reduced_product(hidden, down_weight[0], stages)) * valid_own
        weights = (qfv_weight, out_weight, gate_up_weight, down_weight[0])
        kept = (normed_all, mixed, normed_mid, hidden, pull_mix, pull_mid, pull_act)
        return result.astype(BF16), weights, kept, down_weight[-1], early

    def transposed_sum(left, right, stages):
        half = left.shape[0] // 2
        return collapse(product_t(left[half:], right), product_t(left[:half], right), stages)

    def to_owner(term):
        return lax.psum_scatter(term, "shard", scatter_dimension=0, tiled=True)

    def backward(grad_out, d_down, d_hidden, weights, kept_state, pull_in, earlier):
        qfv_weight, out_weight, gate_up_weight, down_weight = weights
        normed_all, mixed, normed_mid, hidden, pull_mix, pull_mid, pull_act = kept_state
        last = d_hidden is None
        d_out = grad_out * valid_own
        if last:
            d_down, _ = spread_rows(d_out.astype(BF16), stages)
            d_hidden = product_t(d_down, down_weight)
            term_down = weight_term(hidden, d_down)
            earlier, term_down = lax.optimization_barrier((earlier, term_down))
        else:
            term_down = weight_term(hidden, d_down)
            d_hidden, term_down = lax.optimization_barrier((d_hidden, term_down))
        d_gate_up = jnp.concatenate(pull_act(d_hidden), axis=1).astype(BF16)
        term_gate_up = weight_term(normed_mid, d_gate_up)
        d_gate_up, term_gate_up, earlier = lax.optimization_barrier(
            (d_gate_up, term_gate_up, earlier)
        )
        summed_down = to_owner(term_down)
        summed_gate_up = to_owner(term_gate_up)
        more, grad_ffn = pull_mid(transposed_sum(d_gate_up, gate_up_weight, stages))
        d_resid = d_out + more
        d_attn = d_resid.astype(BF16)
        if not last:
            d_attn, summed_down = lax.optimization_barrier((d_attn, summed_down))
        d_attn, _ = spread_rows(d_attn, stages)
        d_mixed = product_t(d_attn, out_weight).reshape(group, length, per_device, head)
        d_q, d_f, d_v, grad_gap, grad_head = pull_mix(d_mixed)
        d_qfv = jnp.stack([d_q, d_f, d_v], axis=2).astype(BF16)
        d_qfv = d_qfv.reshape(group * length, 3 * wide)
        term_out = spread(weight_term(mixed, d_attn)[None], share_stages)
        term_out = term_out[places(share_stages)[jnp.arange(sharing) ^ member]]
        part = model_width // sharing
        term_out = lax.dynamic_slice_in_dim(
            term_out.reshape(sharing * wide, model_width), member * part, part, 1
        )
        term_out = term_out.reshape(shards, each * head, -1, wide).transpose(0, 2, 1, 3)
        term_mix = jnp.concatenate(
            [weight_term(normed_all, d_qfv), term_out.reshape(model_width, wide)], axis=1
        )
        d_qfv, term_mix, summed_gate_up = lax.optimization_barrier(
            (d_qfv, term_mix, summed_gate_up)
        )
        summed_mix = to_owner(term_mix)
        more, grad_mix = pull_in(transposed_sum(d_qfv, qfv_weight, stages))
        d_x = d_resid + more
        small = jnp.zeros((4, model_width), F32).at[0].set(grad_mix).at[1].set(grad_ffn)
        for t in range(per_device):
            column = own_heads[t] * head
            small = lax.dynamic_update_slice(small, grad_head[t][None], (2, column))
            small = lax.dynamic_update_slice(small, grad_gap[t][None], (3, column))
        return d_x, (summed_mix, summed_gate_up, summed_down), small, earlier

    dealt_f32 = dealt.astype(F32)
    normed_first = rms_norm(dealt_f32, gains[0, 0]).astype(BF16)
    _, pull_in_first = jax.vjp(rms_norm, dealt_f32[0], gains[0, 0])
    first, weights_first, kept_first, down_second, d_down_second = forward(
        dealt_f32[0],
        normed_first.reshape(group * length, model_width),
        mix_first,
        gate_up_first,
        gains[0],
        down_pieces=jnp.concatenate([down_first, down_second], axis=0),
    )
    first_f32 = first.astype(F32)
    normed_second, pull_in_second = jax.vjp(rms_norm, first_f32, gains[1, 0])
    second, weights_second, kept_second, _, d_hidden_second = forward(
        first_f32,
        spread_rows(normed_second.astype(BF16), stages)[0],
        mix_second,
        gate_up_second,
        gains[1],
        down_weight=down_second,
    )
    d_first, (mix_1, gate_up_1, down_1), small_second, _ = backward(
        own_cotangent,
        d_down_second,
        d_hidden_second,
        weights_second,
        kept_second,
        pull_in_second,
        (),
    )
    d_dealt, (mix_0, gate_up_0, down_0), small_first, mix_1 = backward(
        d_first.astype(BF16).astype(F32), None, None, weights_first, kept_first, pull_in_first, mix_1
    )

    def begin_collect(of_first, of_second):
        own = jnp.where(on_first, of_first, of_second)
        sent = jnp.where(on_first, of_second, of_first)
        return own, swap(sent, ("section", 1)), swap(own, rep_stages[0])

    def collect(own, other, across):
        blocks = {0: own, reps: other, rep_stages[0][1]: across}
        blocks[reps ^ rep_stages[0][1]] = swap(other, rep_stages[0])
        for stage in rep_stages[1:]:
            blocks.update({code ^ stage[1]: swap(blocks[code], stage) for code in list(blocks)})
        return [blocks[code] for code in range(group)]

    begun = begin_collect(gate_up_0, gate_up_1)
    d_dealt, begun = lax.optimization_barrier((d_dealt, begun))
    gate, up = place_columns(collect(*begun), ident, shards)
    down = place_rows(collect(*begin_collect(down_0, down_1)), ident)

    all_grads = spread(d_dealt.astype(BF16)[None], stages)
    mix_0, all_grads, gate, up, down = lax.optimization_barrier((mix_0, all_grads, gate, up, down))
    inverse = jnp.argsort(block_order)
    own_dealt = lax.dynamic_slice_in_dim(inverse, rep * micro, micro, 0)
    own_holder = (own_dealt % micro) * reps + own_dealt // micro
    back_rows = all_grads[plane_place[own_holder ^ ident]]
    second_rows = jnp.stack([one_way(second, 0), second])
    boundary_out = jnp.where(on_first, back_rows, second_rows).reshape(
        1, micro * length, model_width
    )

    small = jnp.stack([small_first, small_second])
    for stage in stages:
        small = small + swap(small, stage)
    small = jnp.where(on_first, small[0], small[1])
    small = jnp.sum(lax.all_gather(small, "shard", axis=0, tiled=False), axis=0)
    small = lax.dynamic_slice_in_dim(small, shard * local_rows, local_rows, 1)

    sources = [ident ^ code for code in range(group)]
    columns = jnp.stack(
        [head_number(device, t) * head for device in sources for t in range(per_device)]
    )
    corners = []
    for device in sources:
        corners += [device // sharing * each * head, device % sharing * (model_width // sharing)]
    query, forget, into, out = place_mixer(
        collect(*begin_collect(mix_0, mix_1)), columns, jnp.stack(corners), each * head, model_width
    )

    return (
        boundary_out,
        query[None],
        forget[None],
        into[None],
        out[None],
        gate[None],
        up[None],
        down[None],
        small[0][None],
        small[2][None],
        small[1][None],
        small[3][None],
    )


def solution(mesh):
    row_blocks = P("section", ("shard", "rep"), None)
    weight = P("section", "shard", None)
    vector = P("section", "shard")
    return jax.shard_map(
        local,
        mesh=mesh,
        in_specs=(row_blocks, P(("shard", "rep"), None), P(("shard", "rep")))
        + (weight,) * 7
        + (vector,) * 4,
        out_specs=(row_blocks,) + (weight,) * 7 + (vector,) * 4,
        check_vma=False,
    )
```

```python
import functools

import jax
import jax.numpy as jnp
from jax import lax
from jax.experimental import pallas as pl
from jax.experimental.pallas import tpu as pltpu
from jax.sharding import PartitionSpec as P

HEADS = 16
EPS = 1e-06
HEAD_EPS = 0.1
TOP_PRECISION = lax.Precision.HIGHEST
BF16 = jnp.bfloat16
F32 = jnp.float32


def swap(block, stage):
    axis, distance = stage
    return lax.ppermute(block, axis, [(i, i ^ distance) for i in range(lax.axis_size(axis))])


def one_way(block, source):
    return lax.ppermute(block, "section", [(source, 1 - source)])


def spread(block, stages):
    for stage in stages:
        block = jnp.concatenate([block, swap(block, stage)], axis=0)
    return block


def orders(stages):
    outer = stages[:-1]
    turned = outer[1:] + outer[:1]
    codes = []
    for some in (outer, turned):
        order = [0]
        for stage in some:
            order = order + [o ^ (1 << stages.index(stage)) for o in order]
        codes.append(order)
    return outer, turned, codes[0], codes[1]


def blocks_in_order(value, source, target):
    size = value.shape[0] // len(source)
    return jnp.concatenate(
        [value[size * source.index(c) : size * (source.index(c) + 1)] for c in target], axis=0
    )


def join_kernel(order_ref, left, right, far_left, far_right, whole):
    half = left.shape[1]
    whole[0, :, :half] = left[...]
    whole[0, :, half:] = right[...]
    whole[1, :, :half] = far_left[...]
    whole[1, :, half:] = far_right[...]


def join_halves(halves, order):
    rows, half = halves[0].shape
    tile = rows // len(order)
    plain = pl.BlockSpec((tile, half), lambda i, order: (i, 0))
    turned = pl.BlockSpec((tile, half), lambda i, order: (order[i], 0))
    whole = pl.pallas_call(
        join_kernel,
        grid_spec=pltpu.PrefetchScalarGridSpec(
            num_scalar_prefetch=1,
            grid=(len(order),),
            in_specs=[plain, turned, plain, turned],
            out_specs=pl.BlockSpec((2, tile, 2 * half), lambda i, order: (0, i, 0)),
        ),
        out_shape=jax.ShapeDtypeStruct((2, rows, 2 * half), halves[0].dtype),
        compiler_params=pltpu.CompilerParams(vmem_limit_bytes=32 << 20),
    )(jnp.array(order, jnp.int32), *halves)
    return whole.reshape(2 * rows, 2 * half)


def spread_rows(block, stages, tie=None):
    outer, turned, codes, turned_codes = orders(stages)
    half = block.shape[1] // 2
    left, right = block[:, :half], block[:, half:]
    for number, (stage, other) in enumerate(zip(outer, turned)):
        left = jnp.concatenate([left, swap(left, stage)], axis=0)
        right = jnp.concatenate([right, swap(right, other)], axis=0)
        if number == len(outer) - 1 and tie is not None:
            left, right, tie = lax.optimization_barrier((left, right, tie))
    halves = (left, right, swap(left, stages[-1]), swap(right, stages[-1]))
    return join_halves(halves, [turned_codes.index(c) for c in codes]), tie


def collapse(send, keep, stages, tie=None):
    outer, turned, codes, turned_codes = orders(stages)
    total = keep + swap(send.astype(BF16), stages[-1]).astype(F32)
    half = total.shape[1] // 2
    left, right = total[:, :half], blocks_in_order(total[:, half:], codes, turned_codes)
    for stage, other in zip(outer[::-1], turned[::-1]):
        size = left.shape[0] // 2
        left_in = swap(left[size:].astype(BF16), stage)
        right_in = swap(right[size:].astype(BF16), other)
        left = left[:size] + left_in.astype(F32)
        right = right[:size] + right_in.astype(F32)
        if tie is not None:
            left, right, tie = lax.optimization_barrier((left, right, tie))
    return jnp.concatenate([left, right], axis=1), tie


def reduced_product(left, right, stages):
    half = left.shape[0] // 2
    return collapse(product(left[half:], right), product(left[:half], right), stages)[0]


def product(left, right):
    return jnp.dot(left, right, preferred_element_type=F32)


def product_t(left, right):
    return lax.dot_general(left, right, (((1,), (1,)), ((), ())), preferred_element_type=F32)


def weight_term(act_rows, grad_rows):
    return lax.dot_general(
        act_rows, grad_rows, (((0,), (0,)), ((), ())), preferred_element_type=F32
    ).astype(BF16)


def rms_norm(value, gain):
    return value * lax.rsqrt(jnp.mean(value * value, axis=-1, keepdims=True) + EPS) * gain


def head_norm(value, gain):
    return value * lax.rsqrt(jnp.mean(value * value, axis=-1, keepdims=True) + HEAD_EPS) * gain


def segment_info(lens_row, length):
    seg_ends = jnp.cumsum(lens_row)
    position = jnp.arange(length)
    segment_ids = jnp.sum((position[:, None] >= seg_ends[None, :]).astype(jnp.int32), axis=1)
    valid_mask = (position < length - lens_row[-1]).astype(F32)
    return (segment_ids, valid_mask)


def mixer(q, f, v, gap, gain_head, valid_mask, same):
    closed = jax.nn.sigmoid(-f) * gap
    k = closed * valid_mask[:, :, None, None]
    decay = jnp.cumsum(jnp.log(1.0 - closed), axis=1)
    query_decayed = q * jnp.exp(decay)
    key_decayed = k * jnp.exp(-decay)
    scores = (
        jnp.einsum("rthk,rshk->rhts", query_decayed, key_decayed, precision=TOP_PRECISION)
        * same[:, None]
    )
    o = jnp.einsum("rhts,rshv->rthv", scores, v, precision=TOP_PRECISION)
    return head_norm(o, gain_head)


def place_mixer_kernel(wide, columns, corners, *refs):
    sources, (query_ref, forget_ref, input_ref, out_ref) = refs[:-4], refs[-4:]
    step = pl.program_id(0)
    head = wide // (columns.shape[0] // len(sources))
    for j, source in enumerate(sources):
        for kind, target in enumerate((query_ref, forget_ref, input_ref)):
            for t in range(wide // head):
                at = pl.multiple_of(columns[j * (wide // head) + t], head)
                low = kind * wide + t * head
                target[:, pl.ds(at, head)] = source[:, low : low + head].astype(F32)
        row = pl.multiple_of(corners[2 * j], source.shape[0])
        column = pl.multiple_of(corners[2 * j + 1] + step * wide, wide)
        out_ref[pl.ds(row, source.shape[0]), pl.ds(column, wide)] = source[
            :, 3 * wide : 4 * wide
        ].astype(F32)


def place_mixer(sources, columns, corners, tile, model_width):
    rows, total = sources[0].shape
    return pl.pallas_call(
        functools.partial(place_mixer_kernel, total // 4),
        grid_spec=pltpu.PrefetchScalarGridSpec(
            num_scalar_prefetch=2,
            grid=(rows // tile,),
            in_specs=[pl.BlockSpec((tile, total), lambda i, *_: (i, 0))] * len(sources),
            out_specs=[pl.BlockSpec((tile, model_width), lambda i, *_: (i, 0))] * 3
            + [pl.BlockSpec((rows, model_width), lambda i, *_: (0, 0))],
        ),
        out_shape=[jax.ShapeDtypeStruct((rows, model_width), F32)] * 4,
        compiler_params=pltpu.CompilerParams(vmem_limit_bytes=48 << 20),
    )(columns, corners, *sources)


def place_columns_kernel(shards, ident_ref, *refs):
    sources, targets = refs[:-2], refs[-2:]
    values = [source[...] for source in sources]
    bit = 1
    while bit < len(values):
        on = (ident_ref[0] & bit) != 0
        values = [jnp.where(on, values[j ^ bit], values[j]) for j in range(len(values))]
        bit *= 2
    wide = values[0].shape[1] // (2 * shards)
    for kind, target in enumerate(targets):
        parts = []
        for s in range(shards):
            low = (kind * shards + s) * wide
            parts += [value[:, low : low + wide] for value in values]
        target[...] = jnp.concatenate(parts, axis=1).astype(F32)


def place_columns(sources, ident, shards):
    rows, total = sources[0].shape
    tile = 64
    width = len(sources) * total // 2
    return pl.pallas_call(
        functools.partial(place_columns_kernel, shards),
        grid_spec=pltpu.PrefetchScalarGridSpec(
            num_scalar_prefetch=1,
            grid=(rows // tile,),
            in_specs=[pl.BlockSpec((tile, total), lambda i, *_: (i, 0))] * len(sources),
            out_specs=[pl.BlockSpec((tile, width), lambda i, *_: (i, 0))] * 2,
        ),
        out_shape=[jax.ShapeDtypeStruct((rows, width), F32)] * 2,
        compiler_params=pltpu.CompilerParams(vmem_limit_bytes=48 << 20),
    )(ident[None], *sources)


def place_rows_kernel(ident_ref, *refs):
    sources, target = refs[:-1], refs[-1]
    for j, source in enumerate(sources):
        at = pl.multiple_of((ident_ref[0] ^ j) * source.shape[0], 8)
        target[pl.ds(at, source.shape[0]), :] = source[...].astype(F32)


def place_rows(sources, ident):
    rows, width = sources[0].shape
    tile = 512
    return pl.pallas_call(
        place_rows_kernel,
        grid_spec=pltpu.PrefetchScalarGridSpec(
            num_scalar_prefetch=1,
            grid=(width // tile,),
            in_specs=[pl.BlockSpec((rows, tile), lambda i, *_: (0, i))] * len(sources),
            out_specs=pl.BlockSpec((rows * len(sources), tile), lambda i, *_: (0, i)),
        ),
        out_shape=jax.ShapeDtypeStruct((rows * len(sources), width), F32),
        compiler_params=pltpu.CompilerParams(vmem_limit_bytes=48 << 20),
    )(ident[None], *sources)


def split_weights(
    w_query, w_forget, w_input, w_out, w_gate, w_up, w_down, ident, shards, group, sharing
):
    model_width = w_query.shape[1]
    head = model_width // HEADS
    per_device = HEADS // group
    per_shard = HEADS // shards
    cluster, member = ident // sharing, ident % sharing
    each = sharing * per_device // shards

    def head_columns(weight):
        parts = []
        for t in range(per_device):
            at = member * per_device + t
            number = per_shard * (at // each) + cluster * each + at % each
            parts.append(lax.dynamic_slice_in_dim(weight, number * head, head, 1))
        return parts

    width = model_width // sharing
    out = lax.dynamic_slice(
        w_out, (cluster * each * head, member * width), (each * head, width)
    )
    wide = per_device * head
    out = jnp.concatenate([out[:, b : b + wide] for b in range(0, width, wide)], axis=0)
    mix = jnp.concatenate(
        head_columns(w_query) + head_columns(w_forget) + head_columns(w_input) + [out], axis=1
    )
    local_ff = w_down.shape[0]
    own_ff = local_ff // group

    def ff_columns(weight):
        return [
            lax.dynamic_slice_in_dim(weight, local_ff * s + own_ff * ident, own_ff, 1)
            for s in range(shards)
        ]

    gate_up = jnp.concatenate(ff_columns(w_gate) + ff_columns(w_up), axis=1)
    down = lax.dynamic_slice_in_dim(w_down, own_ff * ident, own_ff, 0)
    return (mix, gate_up, down)


def local(
    boundary,
    lengths,
    deal_order,
    w_query,
    w_forget,
    w_input,
    w_out,
    w_gate,
    w_up,
    w_down,
    norm_mix,
    norm_head,
    norm_ffn,
    gate_gap,
):
    micro = deal_order.shape[0]
    reps = lax.axis_size("rep")
    shards = lax.axis_size("shard")
    group = 2 * reps
    model_width = boundary.shape[2]
    length = boundary.shape[1] // micro
    head = model_width // HEADS
    per_device = HEADS // group
    per_shard = HEADS // shards
    sharing = shards * group // HEADS
    each = sharing * per_device // shards
    section = lax.axis_index("section")
    rep = lax.axis_index("rep")
    shard = lax.axis_index("shard")
    on_first = section == 0
    ident = section * reps + rep

    rep_stages = []
    distance = reps // 2
    while distance:
        rep_stages.append(("rep", distance))
        distance //= 2
    stages = [("section", 1)] + rep_stages
    share_stages = [stage for stage in rep_stages if stage[1] < sharing]

    def codes(some):
        order = [0]
        for axis, distance in some:
            bit = reps if axis == "section" else distance
            order = order + [o ^ bit for o in order]
        return order

    def places(some):
        order = codes(some)
        slot = [0] * len(order)
        for at, code in enumerate(order):
            slot[code] = at
        return jnp.array(slot, jnp.int32)

    plane_order = jnp.array(codes(stages), jnp.int32)
    rep_place = places(rep_stages)

    gains = jnp.stack([norm_mix[0], norm_ffn[0], norm_head[0], gate_gap[0]])
    shard_stages = []
    distance = shards // 2
    while distance:
        shard_stages.append(("shard", distance))
        distance //= 2
    gains = spread(gains[None], shard_stages)
    gains = gains[places(shard_stages)[jnp.arange(shards) ^ shard]]
    gains = spread(gains[None], [("section", 1)])[jnp.arange(2) ^ section]

    local_weights = (w_query[0], w_forget[0], w_input[0], w_out[0], w_gate[0], w_up[0], w_down[0])
    kept = split_weights(*local_weights, ident, shards, group, sharing)
    sent = split_weights(
        *local_weights, (1 - section) * reps + rep, shards, group, sharing
    )
    received = [swap(piece, ("section", 1)) for piece in sent]
    kept_mix = kept[0]
    gate_up_first, down_first = [
        jnp.where(on_first, a, b) for a, b in zip(kept[1:], received[1:])
    ]
    gate_up_second, down_second = [
        jnp.where(on_first, b, a) for a, b in zip(kept[1:], received[1:])
    ]

    def over_shard(piece):
        return lax.all_gather(piece, "shard", axis=0, tiled=True)

    member = ident % sharing
    cluster = ident // sharing
    wide = per_device * head
    local_rows = model_width // shards

    kept_mix = over_shard(kept_mix)
    received_mix = over_shard(received[0])
    mix_first = jnp.where(on_first, kept_mix, received_mix)
    mix_second = jnp.where(on_first, received_mix, kept_mix)

    def mixer_weights(mix):
        out = mix[:, 3 * wide :].reshape(shards, -1, each * head, wide)
        out = out.transpose(0, 2, 1, 3).reshape(shards * each * head, model_width // sharing)
        out = spread(out[None], share_stages)
        out = out[places(share_stages)[jnp.arange(sharing) ^ member]]
        out = jnp.swapaxes(out, 0, 1).reshape(shards * each * head, model_width)
        out = lax.dynamic_slice_in_dim(out, member * wide, wide, 0)
        return (mix[:, : 3 * wide], out)

    block_rows = micro * reps
    numbers = jnp.concatenate([deal_order[:, None], lengths], axis=1)
    numbers = spread(numbers[None], rep_stages)[rep_place[jnp.arange(reps) ^ rep]]
    numbers = numbers.reshape(block_rows, -1)
    block_order = numbers[:, 0] % block_rows
    block_lengths = numbers[:, 1:]
    gains = gains.reshape(2, shards, 4, -1).transpose(0, 2, 1, 3).reshape(2, 4, model_width)
    gains = gains.astype(F32)

    def head_number(device, t):
        at = device % sharing * per_device + t
        return per_shard * (at // each) + device // sharing * each + at % each

    own_heads = [head_number(ident, t) for t in range(per_device)]

    def own_channels(vector):
        return jnp.stack(
            [lax.dynamic_slice_in_dim(vector, number * head, head, 0) for number in own_heads]
        )

    holder = plane_order ^ ident
    dealt_row = (holder % reps) * micro + holder // reps
    arrival_row = block_order[dealt_row]
    segment_ids, valid_mask = jax.vmap(lambda lens_row: segment_info(lens_row, length))(
        block_lengths[arrival_row]
    )
    causal = jnp.tril(jnp.ones((length, length), F32))
    same = (segment_ids[:, :, None] == segment_ids[:, None, :]).astype(F32) * causal
    valid_own = valid_mask[0][:, None]

    inverse = lax.dynamic_slice_in_dim(jnp.argsort(block_order), rep * micro, micro, 0)
    back_places = places(rep_stages[:1] + stages[:1] + rep_stages[1:])[
        (inverse % micro * reps + inverse // micro) ^ ident
    ]

    rows = boundary[0].reshape(micro, length, model_width)
    first_rows = jnp.where(on_first, rows, one_way(rows, 0))
    arrivals = spread(first_rows, rep_stages)
    slot = rep_place[(arrival_row // micro) ^ rep] * micro + arrival_row % micro
    dealt = arrivals[slot]
    own_cotangent = jnp.where(on_first, one_way(rows[0], 1), rows[1]).astype(F32)

    d_down_second, _ = spread_rows((own_cotangent * valid_own).astype(BF16), stages)

    def forward(x_own, normed_all, mix, gate_up_piece, gain, down_pieces=None, down_weight=None):
        qfv_weight, out_weight = mixer_weights(mix)
        qfv = product(normed_all, qfv_weight).reshape(group, length, 3, per_device, head)
        mixed, pull_mix = jax.vjp(
            lambda a, b, c, d, e: mixer(a, b, c, d, e, valid_mask, same),
            qfv[:, :, 0],
            qfv[:, :, 1],
            qfv[:, :, 2],
            own_channels(gain[3]),
            own_channels(gain[2]),
        )
        mixed = mixed.reshape(group * length, per_device * head).astype(BF16)
        gate_up_weight, tied = over_shard(gate_up_piece), None
        if down_weight is None:
            mixed, down_pieces = lax.optimization_barrier((mixed, down_pieces))
            down_weight = over_shard(down_pieces[0])
        else:
            tied = product_t(d_down_second, down_weight)
        resid_mid = x_own + reduced_product(mixed, out_weight, stages)
        mid_value, pull_mid = jax.vjp(rms_norm, resid_mid, gain[1])
        normed_mid, tied = spread_rows(mid_value.astype(BF16), stages, tied)
        early = tied
        gate_up = product(normed_mid, gate_up_weight)
        half = gate_up.shape[1] // 2
        hidden, pull_act = jax.vjp(
            lambda a, b: jax.nn.silu(a) * b, gate_up[:, :half], gate_up[:, half:]
        )
        hidden = hidden.astype(BF16)
        later = ()
        if tied is None:
            hidden, early, later = lax.optimization_barrier(
                (hidden, d_down_second, down_pieces[1])
            )
            later = over_shard(later)
        result = (resid_mid + reduced_product(hidden, down_weight, stages)) * valid_own
        weights = (qfv_weight, out_weight, gate_up_weight, down_weight)
        kept = (normed_all, mixed, normed_mid, hidden, pull_mix, pull_mid, pull_act)
        return result.astype(BF16), weights, kept, later, early

    def transposed_sum(left, right, stages, tie=None):
        half = left.shape[0] // 2
        return collapse(product_t(left[half:], right), product_t(left[:half], right), stages, tie)

    def to_owner(term):
        return lax.psum_scatter(term, "shard", scatter_dimension=0, tiled=True)

    def begin_collect(of_first, of_second):
        own = jnp.where(on_first, of_first, of_second)
        sent = jnp.where(on_first, of_second, of_first)
        return own, swap(sent, ("section", 1)), swap(own, rep_stages[0])

    def collect(own, other, across, diagonal=None):
        blocks = {0: own, reps: other, rep_stages[0][1]: across}
        if diagonal is None:
            diagonal = swap(other, rep_stages[0])
        blocks[reps ^ rep_stages[0][1]] = diagonal
        for stage in rep_stages[1:]:
            blocks.update({code ^ stage[1]: swap(blocks[code], stage) for code in list(blocks)})
        return [blocks[code] for code in range(group)]

    def backward(grad_out, d_down, d_hidden, weights, kept_state, pull_in, earlier):
        qfv_weight, out_weight, gate_up_weight, down_weight = weights
        normed_all, mixed, normed_mid, hidden, pull_mix, pull_mid, pull_act = kept_state
        last = d_hidden is None
        d_out = grad_out * valid_own
        if last:
            d_down, _ = spread_rows(d_out.astype(BF16), stages)
            d_hidden = product_t(d_down, down_weight)
        d_gate_up = jnp.concatenate(pull_act(d_hidden), axis=1).astype(BF16)
        term_gate_up = weight_term(normed_mid, d_gate_up)
        if last:
            d_gate_up, term_gate_up, earlier = lax.optimization_barrier(
                (d_gate_up, term_gate_up, earlier)
            )
        else:
            d_gate_up, term_gate_up = lax.optimization_barrier((d_gate_up, term_gate_up))
        summed_gate_up = to_owner(term_gate_up)
        more, grad_ffn = pull_mid(transposed_sum(d_gate_up, gate_up_weight, stages)[0])
        d_resid = d_out + more
        d_attn, term_down = lax.optimization_barrier(
            (d_resid.astype(BF16), weight_term(hidden, d_down))
        )
        summed_down = to_owner(term_down)
        d_attn, _ = spread_rows(d_attn, stages)
        if not last:
            d_attn, summed_gate_up = lax.optimization_barrier((d_attn, summed_gate_up))
        d_mixed = product_t(d_attn, out_weight).reshape(group, length, per_device, head)
        d_q, d_f, d_v, grad_gap, grad_head = pull_mix(d_mixed)
        d_qfv = jnp.stack([d_q, d_f, d_v], axis=2).astype(BF16)
        d_qfv = d_qfv.reshape(group * length, 3 * wide)
        term_out = spread(weight_term(mixed, d_attn)[None], share_stages)
        term_out = term_out[places(share_stages)[jnp.arange(sharing) ^ member]]
        part = model_width // sharing
        term_out = lax.dynamic_slice_in_dim(
            term_out.reshape(sharing * wide, model_width), member * part, part, 1
        )
        term_out = term_out.reshape(shards, each * head, -1, wide).transpose(0, 2, 1, 3)
        term_mix = jnp.concatenate(
            [weight_term(normed_all, d_qfv), term_out.reshape(model_width, wide)], axis=1
        )
        if last:
            d_qfv, term_mix, summed_gate_up = lax.optimization_barrier(
                (d_qfv, term_mix, summed_gate_up)
            )
            begun = begin_collect(summed_gate_up, gate_up_1)
        else:
            d_qfv, term_mix, summed_down, earlier = lax.optimization_barrier(
                (d_qfv, term_mix, summed_down, earlier)
            )
            begun = None
        summed_mix = to_owner(term_mix)
        d_normed, begun = transposed_sum(d_qfv, qfv_weight, stages, begun)
        more, grad_mix = pull_in(d_normed)
        d_x = d_resid + more
        if last:
            summed_gate_up = begun
        small = jnp.zeros((4, model_width), F32).at[0].set(grad_mix).at[1].set(grad_ffn)
        for t in range(per_device):
            column = own_heads[t] * head
            small = lax.dynamic_update_slice(small, grad_head[t][None], (2, column))
            small = lax.dynamic_update_slice(small, grad_gap[t][None], (3, column))
        return d_x, (summed_mix, summed_gate_up, summed_down), small, earlier

    dealt_f32 = dealt.astype(F32)
    normed_first = rms_norm(dealt_f32, gains[0, 0]).astype(BF16)
    _, pull_in_first = jax.vjp(rms_norm, dealt_f32[0], gains[0, 0])
    first, weights_first, kept_first, down_second, d_down_second = forward(
        dealt_f32[0],
        normed_first.reshape(group * length, model_width),
        mix_first,
        gate_up_first,
        gains[0],
        down_pieces=(down_first, down_second),
    )
    first_f32 = first.astype(F32)
    normed_second, pull_in_second = jax.vjp(rms_norm, first_f32, gains[1, 0])
    normed_second, down_second = spread_rows(normed_second.astype(BF16), stages, down_second)
    second, weights_second, kept_second, _, d_hidden_second = forward(
        first_f32,
        normed_second,
        mix_second,
        gate_up_second,
        gains[1],
        down_weight=down_second,
    )
    second_rows = jnp.stack([one_way(second, 0), second])
    d_first, (mix_1, gate_up_1, down_1), small_second, second_rows = backward(
        own_cotangent,
        d_down_second,
        d_hidden_second,
        weights_second,
        kept_second,
        pull_in_second,
        second_rows,
    )
    d_dealt, (mix_0, gate_up_begun, down_0), small_first, mix_1 = backward(
        d_first.astype(BF16).astype(F32), None, None, weights_first, kept_first, pull_in_first, mix_1
    )

    across = rep_stages[0]
    d_dealt, mix_0, gate_up_diagonal, back_places = lax.optimization_barrier(
        (d_dealt, mix_0, swap(gate_up_begun[1], across), back_places)
    )
    mix_own, mix_other, mix_across = begin_collect(mix_0, mix_1)
    rows_sent = [d_dealt, small_first, small_second, jnp.zeros((8, model_width), F32)]
    grads = spread(jnp.concatenate(rows_sent).astype(BF16)[None], rep_stages[:1])
    gate, up = place_columns(collect(*gate_up_begun, gate_up_diagonal), ident, shards)
    down_0, mix_other, mix_across, grads, gate, up = lax.optimization_barrier(
        (down_0, mix_other, mix_across, grads, gate, up)
    )
    down_own, down_other, down_across = begin_collect(down_0, down_1)
    mix_diagonal = swap(mix_other, across)
    down_other, down_across, mix_diagonal, grads = lax.optimization_barrier(
        (down_other, down_across, mix_diagonal, spread(grads, stages[:1]))
    )
    down_diagonal = swap(down_other, across)
    all_grads = spread(grads, rep_stages[1:])
    sources = [ident ^ code for code in range(group)]
    columns = jnp.stack(
        [head_number(device, t) * head for device in sources for t in range(per_device)]
    )
    corners = []
    for device in sources:
        corners += [device // sharing * each * head, device % sharing * (model_width // sharing)]
    query, forget, into, out = place_mixer(
        collect(mix_own, mix_other, mix_across, mix_diagonal),
        columns,
        jnp.stack(corners),
        each * head,
        model_width,
    )
    small = jnp.sum(all_grads[:, length:].astype(F32), axis=0)[:8].reshape(2, 4, model_width)
    small = jnp.where(on_first, small[0], small[1])
    for stage in shard_stages:
        small = small + swap(small, stage)
    small = lax.dynamic_slice_in_dim(small, shard * local_rows, local_rows, 1)

    back_rows = [
        lax.dynamic_slice(all_grads, (back_places[number], 0, 0), (1, length, model_width))
        for number in range(micro)
    ]
    boundary_out = jnp.where(on_first, jnp.concatenate(back_rows), second_rows).reshape(
        1, micro * length, model_width
    )
    mixer_grads = (query, forget, into, out)
    down_diagonal, mixer_grads, boundary_out, small = lax.optimization_barrier(
        (down_diagonal, mixer_grads, boundary_out, small)
    )
    query, forget, into, out = mixer_grads
    down = place_rows(collect(down_own, down_other, down_across, down_diagonal), ident)

    return (
        boundary_out,
        query[None],
        forget[None],
        into[None],
        out[None],
        gate[None],
        up[None],
        down[None],
        small[0][None],
        small[2][None],
        small[1][None],
        small[3][None],
    )


def solution(mesh):
    row_blocks = P("section", ("shard", "rep"), None)
    weight = P("section", "shard", None)
    vector = P("section", "shard")
    return jax.shard_map(
        local,
        mesh=mesh,
        in_specs=(row_blocks, P(("shard", "rep"), None), P(("shard", "rep")))
        + (weight,) * 7
        + (vector,) * 4,
        out_specs=(row_blocks,) + (weight,) * 7 + (vector,) * 4,
        check_vma=False,
    )
```

```python
import functools

import jax
import jax.numpy as jnp
from jax import lax
from jax.experimental import pallas as pl
from jax.experimental.pallas import tpu as pltpu
from jax.sharding import PartitionSpec as P

HEADS = 16
EPS = 1e-06
HEAD_EPS = 0.1
TOP_PRECISION = lax.Precision.HIGHEST
BF16 = jnp.bfloat16
F32 = jnp.float32


def swap(block, stage):
    axis, distance = stage
    return lax.ppermute(block, axis, [(i, i ^ distance) for i in range(lax.axis_size(axis))])


def one_way(block, source):
    return lax.ppermute(block, "section", [(source, 1 - source)])


def spread(block, stages):
    for stage in stages:
        block = jnp.concatenate([block, swap(block, stage)], axis=0)
    return block


def orders(stages):
    outer = stages[:-1]
    turned = outer[1:] + outer[:1]
    codes = []
    for some in (outer, turned):
        order = [0]
        for stage in some:
            order = order + [o ^ (1 << stages.index(stage)) for o in order]
        codes.append(order)
    return outer, turned, codes[0], codes[1]


def blocks_in_order(value, source, target):
    size = value.shape[0] // len(source)
    return jnp.concatenate(
        [value[size * source.index(c) : size * (source.index(c) + 1)] for c in target], axis=0
    )


def join_kernel(order_ref, left, right, far_left, far_right, whole):
    half = left.shape[1]
    whole[0, :, :half] = left[...]
    whole[0, :, half:] = right[...]
    whole[1, :, :half] = far_left[...]
    whole[1, :, half:] = far_right[...]


def join_halves(halves, order):
    rows, half = halves[0].shape
    tile = rows // len(order)
    plain = pl.BlockSpec((tile, half), lambda i, order: (i, 0))
    turned = pl.BlockSpec((tile, half), lambda i, order: (order[i], 0))
    whole = pl.pallas_call(
        join_kernel,
        grid_spec=pltpu.PrefetchScalarGridSpec(
            num_scalar_prefetch=1,
            grid=(len(order),),
            in_specs=[plain, turned, plain, turned],
            out_specs=pl.BlockSpec((2, tile, 2 * half), lambda i, order: (0, i, 0)),
        ),
        out_shape=jax.ShapeDtypeStruct((2, rows, 2 * half), halves[0].dtype),
        compiler_params=pltpu.CompilerParams(vmem_limit_bytes=32 << 20),
    )(jnp.array(order, jnp.int32), *halves)
    return whole.reshape(2 * rows, 2 * half)


def spread_rows(block, stages, tie=None):
    outer, turned, codes, turned_codes = orders(stages)
    half = block.shape[1] // 2
    left, right = block[:, :half], block[:, half:]
    for number, (stage, other) in enumerate(zip(outer, turned)):
        left = jnp.concatenate([left, swap(left, stage)], axis=0)
        right = jnp.concatenate([right, swap(right, other)], axis=0)
        if number == len(outer) - 1 and tie is not None:
            left, right, tie = lax.optimization_barrier((left, right, tie))
    halves = (left, right, swap(left, stages[-1]), swap(right, stages[-1]))
    return join_halves(halves, [turned_codes.index(c) for c in codes]), tie


def collapse(send, keep, stages, tie=None):
    outer, turned, codes, turned_codes = orders(stages)
    total = keep + swap(send.astype(BF16), stages[-1]).astype(F32)
    half = total.shape[1] // 2
    left, right = total[:, :half], blocks_in_order(total[:, half:], codes, turned_codes)
    for stage, other in zip(outer[::-1], turned[::-1]):
        size = left.shape[0] // 2
        left_in = swap(left[size:].astype(BF16), stage)
        right_in = swap(right[size:].astype(BF16), other)
        left = left[:size] + left_in.astype(F32)
        right = right[:size] + right_in.astype(F32)
        if tie is not None:
            left, right, tie = lax.optimization_barrier((left, right, tie))
    return jnp.concatenate([left, right], axis=1), tie


def reduced_product(left, right, stages):
    half = left.shape[0] // 2
    return collapse(product(left[half:], right), product(left[:half], right), stages)[0]


def product(left, right):
    return jnp.dot(left, right, preferred_element_type=F32)


def product_t(left, right):
    return lax.dot_general(left, right, (((1,), (1,)), ((), ())), preferred_element_type=F32)


def weight_term(act_rows, grad_rows):
    return lax.dot_general(
        act_rows, grad_rows, (((0,), (0,)), ((), ())), preferred_element_type=F32
    ).astype(BF16)


def rms_norm(value, gain):
    return value * lax.rsqrt(jnp.mean(value * value, axis=-1, keepdims=True) + EPS) * gain


def head_norm(value, gain):
    return value * lax.rsqrt(jnp.mean(value * value, axis=-1, keepdims=True) + HEAD_EPS) * gain


def segment_info(lens_row, length):
    seg_ends = jnp.cumsum(lens_row)
    position = jnp.arange(length)
    segment_ids = jnp.sum((position[:, None] >= seg_ends[None, :]).astype(jnp.int32), axis=1)
    valid_mask = (position < length - lens_row[-1]).astype(F32)
    return (segment_ids, valid_mask)


def mixer(q, f, v, gap, gain_head, valid_mask, same):
    closed = jax.nn.sigmoid(-f) * gap
    k = closed * valid_mask[:, :, None, None]
    decay = jnp.cumsum(jnp.log(1.0 - closed), axis=1)
    query_decayed = q * jnp.exp(decay)
    key_decayed = k * jnp.exp(-decay)
    scores = (
        jnp.einsum("rthk,rshk->rhts", query_decayed, key_decayed, precision=TOP_PRECISION)
        * same[:, None]
    )
    o = jnp.einsum("rhts,rshv->rthv", scores, v, precision=TOP_PRECISION)
    return head_norm(o, gain_head)


def place_mixer_kernel(wide, columns, corners, *refs):
    sources, (query_ref, forget_ref, input_ref, out_ref) = refs[:-4], refs[-4:]
    step = pl.program_id(0)
    head = wide // (columns.shape[0] // len(sources))
    for j, source in enumerate(sources):
        for kind, target in enumerate((query_ref, forget_ref, input_ref)):
            for t in range(wide // head):
                at = pl.multiple_of(columns[j * (wide // head) + t], head)
                low = kind * wide + t * head
                target[:, pl.ds(at, head)] = source[:, low : low + head].astype(F32)
        row = pl.multiple_of(corners[2 * j], source.shape[0])
        column = pl.multiple_of(corners[2 * j + 1] + step * wide, wide)
        out_ref[pl.ds(row, source.shape[0]), pl.ds(column, wide)] = source[
            :, 3 * wide : 4 * wide
        ].astype(F32)


def place_mixer(sources, columns, corners, tile, model_width):
    rows, total = sources[0].shape
    return pl.pallas_call(
        functools.partial(place_mixer_kernel, total // 4),
        grid_spec=pltpu.PrefetchScalarGridSpec(
            num_scalar_prefetch=2,
            grid=(rows // tile,),
            in_specs=[pl.BlockSpec((tile, total), lambda i, *_: (i, 0))] * len(sources),
            out_specs=[pl.BlockSpec((tile, model_width), lambda i, *_: (i, 0))] * 3
            + [pl.BlockSpec((rows, model_width), lambda i, *_: (0, 0))],
        ),
        out_shape=[jax.ShapeDtypeStruct((rows, model_width), F32)] * 4,
        compiler_params=pltpu.CompilerParams(vmem_limit_bytes=48 << 20),
    )(columns, corners, *sources)


def place_columns_kernel(shards, ident_ref, *refs):
    sources, targets = refs[:-2], refs[-2:]
    values = [source[...] for source in sources]
    bit = 1
    while bit < len(values):
        on = (ident_ref[0] & bit) != 0
        values = [jnp.where(on, values[j ^ bit], values[j]) for j in range(len(values))]
        bit *= 2
    wide = values[0].shape[1] // (2 * shards)
    for kind, target in enumerate(targets):
        parts = []
        for s in range(shards):
            low = (kind * shards + s) * wide
            parts += [value[:, low : low + wide] for value in values]
        target[...] = jnp.concatenate(parts, axis=1).astype(F32)


def place_columns(sources, ident, shards):
    rows, total = sources[0].shape
    tile = 64
    width = len(sources) * total // 2
    return pl.pallas_call(
        functools.partial(place_columns_kernel, shards),
        grid_spec=pltpu.PrefetchScalarGridSpec(
            num_scalar_prefetch=1,
            grid=(rows // tile,),
            in_specs=[pl.BlockSpec((tile, total), lambda i, *_: (i, 0))] * len(sources),
            out_specs=[pl.BlockSpec((tile, width), lambda i, *_: (i, 0))] * 2,
        ),
        out_shape=[jax.ShapeDtypeStruct((rows, width), F32)] * 2,
        compiler_params=pltpu.CompilerParams(vmem_limit_bytes=48 << 20),
    )(ident[None], *sources)


def place_rows_kernel(ident_ref, *refs):
    sources, target = refs[:-1], refs[-1]
    for j, source in enumerate(sources):
        at = pl.multiple_of((ident_ref[0] ^ j) * source.shape[0], 8)
        target[pl.ds(at, source.shape[0]), :] = source[...].astype(F32)


def place_rows(sources, ident):
    rows, width = sources[0].shape
    tile = 512
    return pl.pallas_call(
        place_rows_kernel,
        grid_spec=pltpu.PrefetchScalarGridSpec(
            num_scalar_prefetch=1,
            grid=(width // tile,),
            in_specs=[pl.BlockSpec((rows, tile), lambda i, *_: (0, i))] * len(sources),
            out_specs=pl.BlockSpec((rows * len(sources), tile), lambda i, *_: (0, i)),
        ),
        out_shape=jax.ShapeDtypeStruct((rows * len(sources), width), F32),
        compiler_params=pltpu.CompilerParams(vmem_limit_bytes=48 << 20),
    )(ident[None], *sources)


def split_weights(
    w_query, w_forget, w_input, w_out, w_gate, w_up, w_down, ident, shards, group, sharing
):
    model_width = w_query.shape[1]
    head = model_width // HEADS
    per_device = HEADS // group
    per_shard = HEADS // shards
    cluster, member = ident // sharing, ident % sharing
    each = sharing * per_device // shards

    def head_columns(weight):
        parts = []
        for t in range(per_device):
            at = member * per_device + t
            number = per_shard * (at // each) + cluster * each + at % each
            parts.append(lax.dynamic_slice_in_dim(weight, number * head, head, 1))
        return parts

    width = model_width // sharing
    out = lax.dynamic_slice(
        w_out, (cluster * each * head, member * width), (each * head, width)
    )
    wide = per_device * head
    out = jnp.concatenate([out[:, b : b + wide] for b in range(0, width, wide)], axis=0)
    mix = jnp.concatenate(
        head_columns(w_query) + head_columns(w_forget) + head_columns(w_input) + [out], axis=1
    )
    local_ff = w_down.shape[0]
    own_ff = local_ff // group

    def ff_columns(weight):
        return [
            lax.dynamic_slice_in_dim(weight, local_ff * s + own_ff * ident, own_ff, 1)
            for s in range(shards)
        ]

    gate_up = jnp.concatenate(ff_columns(w_gate) + ff_columns(w_up), axis=1)
    down = lax.dynamic_slice_in_dim(w_down, own_ff * ident, own_ff, 0)
    return (mix, gate_up, down)


def local(
    boundary,
    lengths,
    deal_order,
    w_query,
    w_forget,
    w_input,
    w_out,
    w_gate,
    w_up,
    w_down,
    norm_mix,
    norm_head,
    norm_ffn,
    gate_gap,
):
    micro = deal_order.shape[0]
    reps = lax.axis_size("rep")
    shards = lax.axis_size("shard")
    group = 2 * reps
    model_width = boundary.shape[2]
    length = boundary.shape[1] // micro
    head = model_width // HEADS
    per_device = HEADS // group
    per_shard = HEADS // shards
    sharing = shards * group // HEADS
    each = sharing * per_device // shards
    section = lax.axis_index("section")
    rep = lax.axis_index("rep")
    shard = lax.axis_index("shard")
    on_first = section == 0
    ident = section * reps + rep

    rep_stages = []
    distance = reps // 2
    while distance:
        rep_stages.append(("rep", distance))
        distance //= 2
    stages = [("section", 1)] + rep_stages
    share_stages = [stage for stage in rep_stages if stage[1] < sharing]

    def codes(some):
        order = [0]
        for axis, distance in some:
            bit = reps if axis == "section" else distance
            order = order + [o ^ bit for o in order]
        return order

    def places(some):
        order = codes(some)
        slot = [0] * len(order)
        for at, code in enumerate(order):
            slot[code] = at
        return jnp.array(slot, jnp.int32)

    plane_order = jnp.array(codes(stages), jnp.int32)
    rep_place = places(rep_stages)

    gains = jnp.stack([norm_mix[0], norm_ffn[0], norm_head[0], gate_gap[0]])
    shard_stages = []
    distance = shards // 2
    while distance:
        shard_stages.append(("shard", distance))
        distance //= 2
    gains = spread(gains[None], shard_stages)
    gains = gains[places(shard_stages)[jnp.arange(shards) ^ shard]]
    gains = spread(gains[None], [("section", 1)])[jnp.arange(2) ^ section]

    local_weights = (w_query[0], w_forget[0], w_input[0], w_out[0], w_gate[0], w_up[0], w_down[0])
    kept = split_weights(*local_weights, ident, shards, group, sharing)
    sent = split_weights(
        *local_weights, (1 - section) * reps + rep, shards, group, sharing
    )
    received = [swap(piece, ("section", 1)) for piece in sent]
    kept_mix = kept[0]
    gate_up_first, down_first = [
        jnp.where(on_first, a, b) for a, b in zip(kept[1:], received[1:])
    ]
    gate_up_second, down_second = [
        jnp.where(on_first, b, a) for a, b in zip(kept[1:], received[1:])
    ]

    def over_shard(piece):
        return lax.all_gather(piece, "shard", axis=0, tiled=True)

    member = ident % sharing
    cluster = ident // sharing
    wide = per_device * head
    local_rows = model_width // shards

    kept_mix = over_shard(kept_mix)
    received_mix = over_shard(received[0])
    mix_first = jnp.where(on_first, kept_mix, received_mix)
    mix_second = jnp.where(on_first, received_mix, kept_mix)

    def mixer_weights(mix):
        out = mix[:, 3 * wide :].reshape(shards, -1, each * head, wide)
        out = out.transpose(0, 2, 1, 3).reshape(shards * each * head, model_width // sharing)
        out = spread(out[None], share_stages)
        out = out[places(share_stages)[jnp.arange(sharing) ^ member]]
        out = jnp.swapaxes(out, 0, 1).reshape(shards * each * head, model_width)
        out = lax.dynamic_slice_in_dim(out, member * wide, wide, 0)
        return (mix[:, : 3 * wide], out)

    block_rows = micro * reps
    numbers = jnp.concatenate([deal_order[:, None], lengths], axis=1)
    numbers = spread(numbers[None], rep_stages)[rep_place[jnp.arange(reps) ^ rep]]
    numbers = numbers.reshape(block_rows, -1)
    block_order = numbers[:, 0] % block_rows
    block_lengths = numbers[:, 1:]
    gains = gains.reshape(2, shards, 4, -1).transpose(0, 2, 1, 3).reshape(2, 4, model_width)
    gains = gains.astype(F32)

    def head_number(device, t):
        at = device % sharing * per_device + t
        return per_shard * (at // each) + device // sharing * each + at % each

    own_heads = [head_number(ident, t) for t in range(per_device)]

    def own_channels(vector):
        return jnp.stack(
            [lax.dynamic_slice_in_dim(vector, number * head, head, 0) for number in own_heads]
        )

    holder = plane_order ^ ident
    dealt_row = (holder % reps) * micro + holder // reps
    arrival_row = block_order[dealt_row]
    segment_ids, valid_mask = jax.vmap(lambda lens_row: segment_info(lens_row, length))(
        block_lengths[arrival_row]
    )
    causal = jnp.tril(jnp.ones((length, length), F32))
    same = (segment_ids[:, :, None] == segment_ids[:, None, :]).astype(F32) * causal
    valid_own = valid_mask[0][:, None]

    inverse = lax.dynamic_slice_in_dim(jnp.argsort(block_order), rep * micro, micro, 0)
    back_places = places(rep_stages[:1] + stages[:1] + rep_stages[1:])[
        (inverse % micro * reps + inverse // micro) ^ ident
    ]

    rows = boundary[0].reshape(micro, length, model_width)
    first_rows = jnp.where(on_first, rows, one_way(rows, 0))
    arrivals = spread(first_rows, rep_stages)
    slot = rep_place[(arrival_row // micro) ^ rep] * micro + arrival_row % micro
    dealt = arrivals[slot]
    own_cotangent = jnp.where(on_first, one_way(rows[0], 1), rows[1]).astype(F32)

    d_down_second, _ = spread_rows((own_cotangent * valid_own).astype(BF16), stages)

    def forward(x_own, normed_all, mix, gate_up_piece, gain, down_pieces=None, down_weight=None):
        qfv_weight, out_weight = mixer_weights(mix)
        qfv = product(normed_all, qfv_weight).reshape(group, length, 3, per_device, head)
        mixed, pull_mix = jax.vjp(
            lambda a, b, c, d, e: mixer(a, b, c, d, e, valid_mask, same),
            qfv[:, :, 0],
            qfv[:, :, 1],
            qfv[:, :, 2],
            own_channels(gain[3]),
            own_channels(gain[2]),
        )
        mixed = mixed.reshape(group * length, per_device * head).astype(BF16)
        gate_up_weight, tied = over_shard(gate_up_piece), None
        if down_weight is None:
            mixed, down_pieces = lax.optimization_barrier((mixed, down_pieces))
            down_weight = over_shard(down_pieces[0])
        else:
            tied = product_t(d_down_second, down_weight)
        resid_mid = x_own + reduced_product(mixed, out_weight, stages)
        mid_value, pull_mid = jax.vjp(rms_norm, resid_mid, gain[1])
        normed_mid, tied = spread_rows(mid_value.astype(BF16), stages, tied)
        early = tied
        gate_up = product(normed_mid, gate_up_weight)
        half = gate_up.shape[1] // 2
        hidden, pull_act = jax.vjp(
            lambda a, b: jax.nn.silu(a) * b, gate_up[:, :half], gate_up[:, half:]
        )
        hidden = hidden.astype(BF16)
        later = ()
        if tied is None:
            hidden, early, later = lax.optimization_barrier(
                (hidden, d_down_second, down_pieces[1])
            )
            later = over_shard(later)
        result = (resid_mid + reduced_product(hidden, down_weight, stages)) * valid_own
        weights = (qfv_weight, out_weight, gate_up_weight, down_weight)
        kept = (normed_all, mixed, normed_mid, hidden, pull_mix, pull_mid, pull_act)
        return result.astype(BF16), weights, kept, later, early

    def transposed_sum(left, right, stages, tie=None):
        half = left.shape[0] // 2
        return collapse(product_t(left[half:], right), product_t(left[:half], right), stages, tie)

    def to_owner(term):
        return lax.psum_scatter(term, "shard", scatter_dimension=0, tiled=True)

    def begin_collect(of_first, of_second):
        own = jnp.where(on_first, of_first, of_second)
        sent = jnp.where(on_first, of_second, of_first)
        return own, swap(sent, ("section", 1)), swap(own, rep_stages[0])

    def collect(own, other, across, diagonal=None):
        blocks = {0: own, reps: other, rep_stages[0][1]: across}
        if diagonal is None:
            diagonal = swap(other, rep_stages[0])
        blocks[reps ^ rep_stages[0][1]] = diagonal
        for stage in rep_stages[1:]:
            blocks.update({code ^ stage[1]: swap(blocks[code], stage) for code in list(blocks)})
        return [blocks[code] for code in range(group)]

    def backward(grad_out, d_down, d_hidden, weights, kept_state, pull_in, earlier):
        qfv_weight, out_weight, gate_up_weight, down_weight = weights
        normed_all, mixed, normed_mid, hidden, pull_mix, pull_mid, pull_act = kept_state
        last = d_hidden is None
        d_out = grad_out * valid_own
        if last:
            d_down, _ = spread_rows(d_out.astype(BF16), stages)
            d_hidden = product_t(d_down, down_weight)
        d_gate_up = jnp.concatenate(pull_act(d_hidden), axis=1).astype(BF16)
        term_gate_up = weight_term(normed_mid, d_gate_up)
        if last:
            d_gate_up, term_gate_up, earlier = lax.optimization_barrier(
                (d_gate_up, term_gate_up, earlier)
            )
        else:
            d_gate_up, term_gate_up = lax.optimization_barrier((d_gate_up, term_gate_up))
        summed_gate_up = to_owner(term_gate_up)
        more, grad_ffn = pull_mid(transposed_sum(d_gate_up, gate_up_weight, stages)[0])
        d_resid = d_out + more
        d_attn, term_down = lax.optimization_barrier(
            (d_resid.astype(BF16), weight_term(hidden, d_down))
        )
        summed_down = to_owner(term_down)
        d_attn, _ = spread_rows(d_attn, stages)
        if not last:
            d_attn, summed_gate_up = lax.optimization_barrier((d_attn, summed_gate_up))
        d_mixed = product_t(d_attn, out_weight).reshape(group, length, per_device, head)
        d_q, d_f, d_v, grad_gap, grad_head = pull_mix(d_mixed)
        d_qfv = jnp.stack([d_q, d_f, d_v], axis=2).astype(BF16)
        d_qfv = d_qfv.reshape(group * length, 3 * wide)
        term_out = spread(weight_term(mixed, d_attn)[None], share_stages)
        term_out = term_out[places(share_stages)[jnp.arange(sharing) ^ member]]
        part = model_width // sharing
        term_out = lax.dynamic_slice_in_dim(
            term_out.reshape(sharing * wide, model_width), member * part, part, 1
        )
        term_out = term_out.reshape(shards, each * head, -1, wide).transpose(0, 2, 1, 3)
        term_mix = jnp.concatenate(
            [weight_term(normed_all, d_qfv), term_out.reshape(model_width, wide)], axis=1
        )
        if last:
            d_qfv, term_mix, summed_gate_up = lax.optimization_barrier(
                (d_qfv, term_mix, summed_gate_up)
            )
            begun = begin_collect(summed_gate_up, gate_up_1)
        else:
            d_qfv, term_mix, summed_down, earlier = lax.optimization_barrier(
                (d_qfv, term_mix, summed_down, earlier)
            )
            begun = None
        summed_mix = to_owner(term_mix)
        d_normed, begun = transposed_sum(d_qfv, qfv_weight, stages, begun)
        more, grad_mix = pull_in(d_normed)
        d_x = d_resid + more
        if last:
            summed_gate_up = begun
        small = jnp.zeros((4, model_width), F32).at[0].set(grad_mix).at[1].set(grad_ffn)
        for t in range(per_device):
            column = own_heads[t] * head
            small = lax.dynamic_update_slice(small, grad_head[t][None], (2, column))
            small = lax.dynamic_update_slice(small, grad_gap[t][None], (3, column))
        return d_x, (summed_mix, summed_gate_up, summed_down), small, earlier

    dealt_f32 = dealt.astype(F32)
    normed_first = rms_norm(dealt_f32, gains[0, 0]).astype(BF16)
    _, pull_in_first = jax.vjp(rms_norm, dealt_f32[0], gains[0, 0])
    first, weights_first, kept_first, down_second, d_down_second = forward(
        dealt_f32[0],
        normed_first.reshape(group * length, model_width),
        mix_first,
        gate_up_first,
        gains[0],
        down_pieces=(down_first, down_second),
    )
    first_f32 = first.astype(F32)
    normed_second, pull_in_second = jax.vjp(rms_norm, first_f32, gains[1, 0])
    normed_second, down_second = spread_rows(normed_second.astype(BF16), stages, down_second)
    second, weights_second, kept_second, _, d_hidden_second = forward(
        first_f32,
        normed_second,
        mix_second,
        gate_up_second,
        gains[1],
        down_weight=down_second,
    )
    second_rows = jnp.stack([one_way(second, 0), second])
    d_first, (mix_1, gate_up_1, down_1), small_second, second_rows = backward(
        own_cotangent,
        d_down_second,
        d_hidden_second,
        weights_second,
        kept_second,
        pull_in_second,
        second_rows,
    )
    d_dealt, (mix_0, gate_up_begun, down_0), small_first, mix_1 = backward(
        d_first.astype(BF16).astype(F32), None, None, weights_first, kept_first, pull_in_first, mix_1
    )

    across = rep_stages[0]
    small = jnp.concatenate([small_first, small_second])
    for stage in shard_stages:
        small = small + swap(small, stage)
    d_dealt, mix_0, gate_up_diagonal, back_places, small = lax.optimization_barrier(
        (d_dealt, mix_0, swap(gate_up_begun[1], across), back_places, small)
    )
    mix_own, mix_other, mix_across = begin_collect(mix_0, mix_1)
    rows_sent = [d_dealt, small, jnp.zeros((8, model_width), F32)]
    grads = spread(jnp.concatenate(rows_sent).astype(BF16)[None], rep_stages[:1])
    gate, up = place_columns(collect(*gate_up_begun, gate_up_diagonal), ident, shards)
    down_0, mix_other, mix_across, grads, gate, up = lax.optimization_barrier(
        (down_0, mix_other, mix_across, grads, gate, up)
    )
    down_own, down_other, down_across = begin_collect(down_0, down_1)
    mix_diagonal = swap(mix_other, across)
    down_other, down_across, mix_diagonal, grads = lax.optimization_barrier(
        (down_other, down_across, mix_diagonal, spread(grads, stages[:1]))
    )
    down_diagonal = swap(down_other, across)
    grads = spread(grads, rep_stages[1:-1])
    far_grads = swap(grads, stages[-1])
    sources = [ident ^ code for code in range(group)]
    columns = jnp.stack(
        [head_number(device, t) * head for device in sources for t in range(per_device)]
    )
    corners = []
    for device in sources:
        corners += [device // sharing * each * head, device % sharing * (model_width // sharing)]
    query, forget, into, out = place_mixer(
        collect(mix_own, mix_other, mix_across, mix_diagonal),
        columns,
        jnp.stack(corners),
        each * head,
        model_width,
    )
    small = jnp.sum(grads[:, length:].astype(F32), axis=0)
    small = (small + jnp.sum(far_grads[:, length:].astype(F32), axis=0))[:8]
    small = lax.dynamic_slice(
        small, (4 * section, shard * local_rows), (4, local_rows)
    )

    near_count = grads.shape[0]
    back_rows = []
    for number in range(micro):
        place = back_places[number]
        start = (place % near_count, 0, 0)
        near, far = [
            lax.dynamic_slice(value, start, (1, length, model_width))
            for value in (grads, far_grads)
        ]
        back_rows.append(jnp.where(place < near_count, near, far))
    boundary_out = jnp.where(on_first, jnp.concatenate(back_rows), second_rows).reshape(
        1, micro * length, model_width
    )
    mixer_grads = (query, forget, into, out)
    down_diagonal, mixer_grads, boundary_out, small = lax.optimization_barrier(
        (down_diagonal, mixer_grads, boundary_out, small)
    )
    query, forget, into, out = mixer_grads
    down = place_rows(collect(down_own, down_other, down_across, down_diagonal), ident)

    return (
        boundary_out,
        query[None],
        forget[None],
        into[None],
        out[None],
        gate[None],
        up[None],
        down[None],
        small[0][None],
        small[2][None],
        small[1][None],
        small[3][None],
    )


def solution(mesh):
    row_blocks = P("section", ("shard", "rep"), None)
    weight = P("section", "shard", None)
    vector = P("section", "shard")
    return jax.shard_map(
        local,
        mesh=mesh,
        in_specs=(row_blocks, P(("shard", "rep"), None), P(("shard", "rep")))
        + (weight,) * 7
        + (vector,) * 4,
        out_specs=(row_blocks,) + (weight,) * 7 + (vector,) * 4,
        check_vma=False,
    )
```

```python
import functools

import jax
import jax.numpy as jnp
from jax import lax
from jax.experimental import pallas as pl
from jax.experimental.pallas import tpu as pltpu
from jax.sharding import PartitionSpec as P

HEADS = 16
EPS = 1e-06
HEAD_EPS = 0.1
TOP_PRECISION = lax.Precision.HIGHEST
BF16 = jnp.bfloat16
F32 = jnp.float32


def swap(block, stage):
    axis, distance = stage
    return lax.ppermute(block, axis, [(i, i ^ distance) for i in range(lax.axis_size(axis))])


def one_way(block, source):
    return lax.ppermute(block, "section", [(source, 1 - source)])


def spread(block, stages):
    for stage in stages:
        block = jnp.concatenate([block, swap(block, stage)], axis=0)
    return block


def orders(stages):
    outer = stages[:-1]
    turned = outer[1:] + outer[:1]
    codes = []
    for some in (outer, turned):
        order = [0]
        for stage in some:
            order = order + [o ^ (1 << stages.index(stage)) for o in order]
        codes.append(order)
    return outer, turned, codes[0], codes[1]


def blocks_in_order(value, source, target):
    size = value.shape[0] // len(source)
    return jnp.concatenate(
        [value[size * source.index(c) : size * (source.index(c) + 1)] for c in target], axis=0
    )


def join_kernel(order_ref, left, right, far_left, far_right, whole):
    half = left.shape[1]
    whole[0, :, :half] = left[...]
    whole[0, :, half:] = right[...]
    whole[1, :, :half] = far_left[...]
    whole[1, :, half:] = far_right[...]


def join_halves(halves, order):
    rows, half = halves[0].shape
    tile = rows // len(order)
    plain = pl.BlockSpec((tile, half), lambda i, order: (i, 0))
    turned = pl.BlockSpec((tile, half), lambda i, order: (order[i], 0))
    whole = pl.pallas_call(
        join_kernel,
        grid_spec=pltpu.PrefetchScalarGridSpec(
            num_scalar_prefetch=1,
            grid=(len(order),),
            in_specs=[plain, turned, plain, turned],
            out_specs=pl.BlockSpec((2, tile, 2 * half), lambda i, order: (0, i, 0)),
        ),
        out_shape=jax.ShapeDtypeStruct((2, rows, 2 * half), halves[0].dtype),
        compiler_params=pltpu.CompilerParams(vmem_limit_bytes=32 << 20),
    )(jnp.array(order, jnp.int32), *halves)
    return whole.reshape(2 * rows, 2 * half)


def spread_rows(block, stages, tie=None):
    outer, turned, codes, turned_codes = orders(stages)
    half = block.shape[1] // 2
    left, right = block[:, :half], block[:, half:]
    for number, (stage, other) in enumerate(zip(outer, turned)):
        left = jnp.concatenate([left, swap(left, stage)], axis=0)
        right = jnp.concatenate([right, swap(right, other)], axis=0)
        if number == len(outer) - 1 and tie is not None:
            left, right, tie = lax.optimization_barrier((left, right, tie))
    halves = (left, right, swap(left, stages[-1]), swap(right, stages[-1]))
    return join_halves(halves, [turned_codes.index(c) for c in codes]), tie


def collapse(send, keep, stages, tie=None):
    outer, turned, codes, turned_codes = orders(stages)
    total = keep + swap(send.astype(BF16), stages[-1]).astype(F32)
    half = total.shape[1] // 2
    left, right = total[:, :half], blocks_in_order(total[:, half:], codes, turned_codes)
    for stage, other in zip(outer[::-1], turned[::-1]):
        size = left.shape[0] // 2
        left_in = swap(left[size:].astype(BF16), stage)
        right_in = swap(right[size:].astype(BF16), other)
        left = left[:size] + left_in.astype(F32)
        right = right[:size] + right_in.astype(F32)
        if tie is not None:
            left, right, tie = lax.optimization_barrier((left, right, tie))
    return jnp.concatenate([left, right], axis=1), tie


def reduced_product(left, right, stages):
    half = left.shape[0] // 2
    return collapse(product(left[half:], right), product(left[:half], right), stages)[0]


def product(left, right):
    return jnp.dot(left, right, preferred_element_type=F32)


def product_t(left, right):
    return lax.dot_general(left, right, (((1,), (1,)), ((), ())), preferred_element_type=F32)


def weight_term(act_rows, grad_rows):
    return lax.dot_general(
        act_rows, grad_rows, (((0,), (0,)), ((), ())), preferred_element_type=F32
    ).astype(BF16)


def rms_norm(value, gain):
    return value * lax.rsqrt(jnp.mean(value * value, axis=-1, keepdims=True) + EPS) * gain


def head_norm(value, gain):
    return value * lax.rsqrt(jnp.mean(value * value, axis=-1, keepdims=True) + HEAD_EPS) * gain


def segment_info(lens_row, length):
    seg_ends = jnp.cumsum(lens_row)
    position = jnp.arange(length)
    segment_ids = jnp.sum((position[:, None] >= seg_ends[None, :]).astype(jnp.int32), axis=1)
    valid_mask = (position < length - lens_row[-1]).astype(F32)
    return (segment_ids, valid_mask)


def mixer(q, f, v, gap, gain_head, valid_mask, same):
    closed = jax.nn.sigmoid(-f) * gap
    k = closed * valid_mask[:, :, None, None]
    decay = jnp.cumsum(jnp.log(1.0 - closed), axis=1)
    query_decayed = q * jnp.exp(decay)
    key_decayed = k * jnp.exp(-decay)
    scores = (
        jnp.einsum("rthk,rshk->rhts", query_decayed, key_decayed, precision=TOP_PRECISION)
        * same[:, None]
    )
    o = jnp.einsum("rhts,rshv->rthv", scores, v, precision=TOP_PRECISION)
    return head_norm(o, gain_head)


def place_mixer_kernel(wide, columns, corners, *refs):
    sources, (query_ref, forget_ref, input_ref, out_ref) = refs[:-4], refs[-4:]
    step = pl.program_id(0)
    head = wide // (columns.shape[0] // len(sources))
    for j, source in enumerate(sources):
        for kind, target in enumerate((query_ref, forget_ref, input_ref)):
            for t in range(wide // head):
                at = pl.multiple_of(columns[j * (wide // head) + t], head)
                low = kind * wide + t * head
                target[:, pl.ds(at, head)] = source[:, low : low + head].astype(F32)
        row = pl.multiple_of(corners[2 * j], source.shape[0])
        column = pl.multiple_of(corners[2 * j + 1] + step * wide, wide)
        out_ref[pl.ds(row, source.shape[0]), pl.ds(column, wide)] = source[
            :, 3 * wide : 4 * wide
        ].astype(F32)


def place_mixer(sources, columns, corners, tile, model_width):
    rows, total = sources[0].shape
    return pl.pallas_call(
        functools.partial(place_mixer_kernel, total // 4),
        grid_spec=pltpu.PrefetchScalarGridSpec(
            num_scalar_prefetch=2,
            grid=(rows // tile,),
            in_specs=[pl.BlockSpec((tile, total), lambda i, *_: (i, 0))] * len(sources),
            out_specs=[pl.BlockSpec((tile, model_width), lambda i, *_: (i, 0))] * 3
            + [pl.BlockSpec((rows, model_width), lambda i, *_: (0, 0))],
        ),
        out_shape=[jax.ShapeDtypeStruct((rows, model_width), F32)] * 4,
        compiler_params=pltpu.CompilerParams(vmem_limit_bytes=48 << 20),
    )(columns, corners, *sources)


def place_columns_kernel(shards, ident_ref, *refs):
    sources, targets = refs[:-2], refs[-2:]
    values = [source[...] for source in sources]
    bit = 1
    while bit < len(values):
        on = (ident_ref[0] & bit) != 0
        values = [jnp.where(on, values[j ^ bit], values[j]) for j in range(len(values))]
        bit *= 2
    wide = values[0].shape[1] // (2 * shards)
    for kind, target in enumerate(targets):
        parts = []
        for s in range(shards):
            low = (kind * shards + s) * wide
            parts += [value[:, low : low + wide] for value in values]
        target[...] = jnp.concatenate(parts, axis=1).astype(F32)


def place_columns(sources, ident, shards):
    rows, total = sources[0].shape
    tile = 64
    width = len(sources) * total // 2
    return pl.pallas_call(
        functools.partial(place_columns_kernel, shards),
        grid_spec=pltpu.PrefetchScalarGridSpec(
            num_scalar_prefetch=1,
            grid=(rows // tile,),
            in_specs=[pl.BlockSpec((tile, total), lambda i, *_: (i, 0))] * len(sources),
            out_specs=[pl.BlockSpec((tile, width), lambda i, *_: (i, 0))] * 2,
        ),
        out_shape=[jax.ShapeDtypeStruct((rows, width), F32)] * 2,
        compiler_params=pltpu.CompilerParams(vmem_limit_bytes=48 << 20),
    )(ident[None], *sources)


def place_rows_kernel(ident_ref, *refs):
    sources, target = refs[:-1], refs[-1]
    for j, source in enumerate(sources):
        at = pl.multiple_of((ident_ref[0] ^ j) * source.shape[0], 8)
        target[pl.ds(at, source.shape[0]), :] = source[...].astype(F32)


def place_rows(sources, ident):
    rows, width = sources[0].shape
    tile = 512
    return pl.pallas_call(
        place_rows_kernel,
        grid_spec=pltpu.PrefetchScalarGridSpec(
            num_scalar_prefetch=1,
            grid=(width // tile,),
            in_specs=[pl.BlockSpec((rows, tile), lambda i, *_: (0, i))] * len(sources),
            out_specs=pl.BlockSpec((rows * len(sources), tile), lambda i, *_: (0, i)),
        ),
        out_shape=jax.ShapeDtypeStruct((rows * len(sources), width), F32),
        compiler_params=pltpu.CompilerParams(vmem_limit_bytes=48 << 20),
    )(ident[None], *sources)


def split_weights(
    w_query, w_forget, w_input, w_out, w_gate, w_up, w_down, ident, shards, group, sharing
):
    model_width = w_query.shape[1]
    head = model_width // HEADS
    per_device = HEADS // group
    per_shard = HEADS // shards
    cluster, member = ident // sharing, ident % sharing
    each = sharing * per_device // shards

    def head_columns(weight):
        parts = []
        for t in range(per_device):
            at = member * per_device + t
            number = per_shard * (at // each) + cluster * each + at % each
            parts.append(lax.dynamic_slice_in_dim(weight, number * head, head, 1))
        return parts

    width = model_width // sharing
    out = lax.dynamic_slice(
        w_out, (cluster * each * head, member * width), (each * head, width)
    )
    wide = per_device * head
    out = jnp.concatenate([out[:, b : b + wide] for b in range(0, width, wide)], axis=0)
    mix = jnp.concatenate(
        head_columns(w_query) + head_columns(w_forget) + head_columns(w_input) + [out], axis=1
    )
    local_ff = w_down.shape[0]
    own_ff = local_ff // group

    def ff_columns(weight):
        return [
            lax.dynamic_slice_in_dim(weight, local_ff * s + own_ff * ident, own_ff, 1)
            for s in range(shards)
        ]

    gate_up = jnp.concatenate(ff_columns(w_gate) + ff_columns(w_up), axis=1)
    down = lax.dynamic_slice_in_dim(w_down, own_ff * ident, own_ff, 0)
    return (mix, gate_up, down)


def local(
    boundary,
    lengths,
    deal_order,
    w_query,
    w_forget,
    w_input,
    w_out,
    w_gate,
    w_up,
    w_down,
    norm_mix,
    norm_head,
    norm_ffn,
    gate_gap,
):
    micro = deal_order.shape[0]
    reps = lax.axis_size("rep")
    shards = lax.axis_size("shard")
    group = 2 * reps
    model_width = boundary.shape[2]
    length = boundary.shape[1] // micro
    head = model_width // HEADS
    per_device = HEADS // group
    per_shard = HEADS // shards
    sharing = shards * group // HEADS
    each = sharing * per_device // shards
    section = lax.axis_index("section")
    rep = lax.axis_index("rep")
    shard = lax.axis_index("shard")
    on_first = section == 0
    ident = section * reps + rep

    rep_stages = []
    distance = reps // 2
    while distance:
        rep_stages.append(("rep", distance))
        distance //= 2
    stages = [("section", 1)] + rep_stages
    share_stages = [stage for stage in rep_stages if stage[1] < sharing]

    def codes(some):
        order = [0]
        for axis, distance in some:
            bit = reps if axis == "section" else distance
            order = order + [o ^ bit for o in order]
        return order

    def places(some):
        order = codes(some)
        slot = [0] * len(order)
        for at, code in enumerate(order):
            slot[code] = at
        return jnp.array(slot, jnp.int32)

    plane_order = jnp.array(codes(stages), jnp.int32)
    rep_place = places(rep_stages)

    gains = jnp.stack([norm_mix[0], norm_ffn[0], norm_head[0], gate_gap[0]])
    shard_stages = []
    distance = shards // 2
    while distance:
        shard_stages.append(("shard", distance))
        distance //= 2
    gains = spread(gains[None], shard_stages)
    gains = gains[places(shard_stages)[jnp.arange(shards) ^ shard]]
    gains = spread(gains[None], [("section", 1)])[jnp.arange(2) ^ section]

    local_weights = (w_query[0], w_forget[0], w_input[0], w_out[0], w_gate[0], w_up[0], w_down[0])
    kept = split_weights(*local_weights, ident, shards, group, sharing)
    sent = split_weights(
        *local_weights, (1 - section) * reps + rep, shards, group, sharing
    )
    received = [swap(piece, ("section", 1)) for piece in sent]
    kept_mix = kept[0]
    gate_up_first, down_first = [
        jnp.where(on_first, a, b) for a, b in zip(kept[1:], received[1:])
    ]
    gate_up_second, down_second = [
        jnp.where(on_first, b, a) for a, b in zip(kept[1:], received[1:])
    ]

    def over_shard(piece):
        return lax.all_gather(piece, "shard", axis=0, tiled=True)

    member = ident % sharing
    cluster = ident // sharing
    wide = per_device * head
    local_rows = model_width // shards

    kept_mix = over_shard(kept_mix)
    received_mix = over_shard(received[0])
    mix_first = jnp.where(on_first, kept_mix, received_mix)
    mix_second = jnp.where(on_first, received_mix, kept_mix)

    def mixer_weights(mix):
        out = mix[:, 3 * wide :].reshape(shards, -1, each * head, wide)
        out = out.transpose(0, 2, 1, 3).reshape(shards * each * head, model_width // sharing)
        out = spread(out[None], share_stages)
        out = out[places(share_stages)[jnp.arange(sharing) ^ member]]
        out = jnp.swapaxes(out, 0, 1).reshape(shards * each * head, model_width)
        out = lax.dynamic_slice_in_dim(out, member * wide, wide, 0)
        return (mix[:, : 3 * wide], out)

    block_rows = micro * reps
    numbers = jnp.concatenate([deal_order[:, None], lengths], axis=1)
    numbers = spread(numbers[None], rep_stages)[rep_place[jnp.arange(reps) ^ rep]]
    numbers = numbers.reshape(block_rows, -1)
    block_order = numbers[:, 0] % block_rows
    block_lengths = numbers[:, 1:]
    gains = gains.reshape(2, shards, 4, -1).transpose(0, 2, 1, 3).reshape(2, 4, model_width)
    gains = gains.astype(F32)

    def head_number(device, t):
        at = device % sharing * per_device + t
        return per_shard * (at // each) + device // sharing * each + at % each

    own_heads = [head_number(ident, t) for t in range(per_device)]

    def own_channels(vector):
        return jnp.stack(
            [lax.dynamic_slice_in_dim(vector, number * head, head, 0) for number in own_heads]
        )

    holder = plane_order ^ ident
    dealt_row = (holder % reps) * micro + holder // reps
    arrival_row = block_order[dealt_row]
    segment_ids, valid_mask = jax.vmap(lambda lens_row: segment_info(lens_row, length))(
        block_lengths[arrival_row]
    )
    causal = jnp.tril(jnp.ones((length, length), F32))
    same = (segment_ids[:, :, None] == segment_ids[:, None, :]).astype(F32) * causal
    valid_own = valid_mask[0][:, None]

    inverse = lax.dynamic_slice_in_dim(jnp.argsort(block_order), rep * micro, micro, 0)
    back_places = places(rep_stages[:1] + stages[:1] + rep_stages[1:])[
        (inverse % micro * reps + inverse // micro) ^ ident
    ]

    rows = boundary[0].reshape(micro, length, model_width)
    first_rows = jnp.where(on_first, rows, one_way(rows, 0))
    arrivals = spread(first_rows, rep_stages)
    slot = rep_place[(arrival_row // micro) ^ rep] * micro + arrival_row % micro
    dealt = arrivals[slot]
    own_cotangent = jnp.where(on_first, one_way(rows[0], 1), rows[1]).astype(F32)

    d_down_second, _ = spread_rows((own_cotangent * valid_own).astype(BF16), stages)

    def forward(x_own, normed_all, mix, gate_up_piece, gain, down_pieces=None, down_weight=None):
        qfv_weight, out_weight = mixer_weights(mix)
        qfv = product(normed_all, qfv_weight).reshape(group, length, 3, per_device, head)
        mixed, pull_mix = jax.vjp(
            lambda a, b, c, d, e: mixer(a, b, c, d, e, valid_mask, same),
            qfv[:, :, 0],
            qfv[:, :, 1],
            qfv[:, :, 2],
            own_channels(gain[3]),
            own_channels(gain[2]),
        )
        mixed = mixed.reshape(group * length, per_device * head).astype(BF16)
        gate_up_weight, tied = over_shard(gate_up_piece), None
        if down_weight is None:
            mixed, down_pieces = lax.optimization_barrier((mixed, down_pieces))
            down_weight = over_shard(down_pieces[0])
        else:
            tied = product_t(d_down_second, down_weight)
        resid_mid = x_own + reduced_product(mixed, out_weight, stages)
        mid_value, pull_mid = jax.vjp(rms_norm, resid_mid, gain[1])
        normed_mid, tied = spread_rows(mid_value.astype(BF16), stages, tied)
        early = tied
        gate_up = product(normed_mid, gate_up_weight)
        half = gate_up.shape[1] // 2
        hidden, pull_act = jax.vjp(
            lambda a, b: jax.nn.silu(a) * b, gate_up[:, :half], gate_up[:, half:]
        )
        hidden = hidden.astype(BF16)
        later = ()
        if tied is None:
            hidden, early, later = lax.optimization_barrier(
                (hidden, d_down_second, down_pieces[1])
            )
            later = over_shard(later)
        result = (resid_mid + reduced_product(hidden, down_weight, stages)) * valid_own
        weights = (qfv_weight, out_weight, gate_up_weight, down_weight)
        kept = (normed_all, mixed, normed_mid, hidden, pull_mix, pull_mid, pull_act)
        return result.astype(BF16), weights, kept, later, early

    def transposed_sum(left, right, stages, tie=None):
        half = left.shape[0] // 2
        return collapse(product_t(left[half:], right), product_t(left[:half], right), stages, tie)

    def to_owner(term):
        return lax.psum_scatter(term, "shard", scatter_dimension=0, tiled=True)

    def begin_collect(of_first, of_second):
        own = jnp.where(on_first, of_first, of_second)
        sent = jnp.where(on_first, of_second, of_first)
        return own, swap(sent, ("section", 1)), swap(own, rep_stages[0])

    def collect(own, other, across, diagonal=None):
        blocks = {0: own, reps: other, rep_stages[0][1]: across}
        if diagonal is None:
            diagonal = swap(other, rep_stages[0])
        blocks[reps ^ rep_stages[0][1]] = diagonal
        for stage in rep_stages[1:]:
            blocks.update({code ^ stage[1]: swap(blocks[code], stage) for code in list(blocks)})
        return [blocks[code] for code in range(group)]

    def backward(grad_out, d_down, d_hidden, weights, kept_state, pull_in, earlier):
        qfv_weight, out_weight, gate_up_weight, down_weight = weights
        normed_all, mixed, normed_mid, hidden, pull_mix, pull_mid, pull_act = kept_state
        last = d_hidden is None
        d_out = grad_out * valid_own
        if last:
            d_down, _ = spread_rows(d_out.astype(BF16), stages)
            d_hidden = product_t(d_down, down_weight)
        d_gate_up = jnp.concatenate(pull_act(d_hidden), axis=1).astype(BF16)
        term_gate_up = weight_term(normed_mid, d_gate_up)
        if last:
            d_gate_up, term_gate_up, earlier = lax.optimization_barrier(
                (d_gate_up, term_gate_up, earlier)
            )
        else:
            d_gate_up, term_gate_up = lax.optimization_barrier((d_gate_up, term_gate_up))
        summed_gate_up = to_owner(term_gate_up)
        more, grad_ffn = pull_mid(transposed_sum(d_gate_up, gate_up_weight, stages)[0])
        d_resid = d_out + more
        d_attn, term_down = lax.optimization_barrier(
            (d_resid.astype(BF16), weight_term(hidden, d_down))
        )
        summed_down = to_owner(term_down)
        d_attn, _ = spread_rows(d_attn, stages)
        if not last:
            d_attn, summed_gate_up = lax.optimization_barrier((d_attn, summed_gate_up))
        d_mixed = product_t(d_attn, out_weight).reshape(group, length, per_device, head)
        d_q, d_f, d_v, grad_gap, grad_head = pull_mix(d_mixed)
        d_qfv = jnp.stack([d_q, d_f, d_v], axis=2).astype(BF16)
        d_qfv = d_qfv.reshape(group * length, 3 * wide)
        term_out = spread(weight_term(mixed, d_attn)[None], share_stages)
        term_out = term_out[places(share_stages)[jnp.arange(sharing) ^ member]]
        part = model_width // sharing
        term_out = lax.dynamic_slice_in_dim(
            term_out.reshape(sharing * wide, model_width), member * part, part, 1
        )
        term_out = term_out.reshape(shards, each * head, -1, wide).transpose(0, 2, 1, 3)
        term_mix = jnp.concatenate(
            [weight_term(normed_all, d_qfv), term_out.reshape(model_width, wide)], axis=1
        )
        if last:
            d_qfv, term_mix, summed_gate_up = lax.optimization_barrier(
                (d_qfv, term_mix, summed_gate_up)
            )
            begun = begin_collect(summed_gate_up, gate_up_1)
        else:
            d_qfv, term_mix, summed_down, earlier = lax.optimization_barrier(
                (d_qfv, term_mix, summed_down, earlier)
            )
            begun = None
        summed_mix = to_owner(term_mix)
        d_normed, begun = transposed_sum(d_qfv, qfv_weight, stages, begun)
        more, grad_mix = pull_in(d_normed)
        d_x = d_resid + more
        if last:
            summed_gate_up = begun
        small = jnp.zeros((4, model_width), F32).at[0].set(grad_mix).at[1].set(grad_ffn)
        for t in range(per_device):
            column = own_heads[t] * head
            small = lax.dynamic_update_slice(small, grad_head[t][None], (2, column))
            small = lax.dynamic_update_slice(small, grad_gap[t][None], (3, column))
        return d_x, (summed_mix, summed_gate_up, summed_down), small, earlier

    dealt_f32 = dealt.astype(F32)
    normed_first = rms_norm(dealt_f32, gains[0, 0]).astype(BF16)
    _, pull_in_first = jax.vjp(rms_norm, dealt_f32[0], gains[0, 0])
    first, weights_first, kept_first, down_second, d_down_second = forward(
        dealt_f32[0],
        normed_first.reshape(group * length, model_width),
        mix_first,
        gate_up_first,
        gains[0],
        down_pieces=(down_first, down_second),
    )
    first_f32 = first.astype(F32)
    normed_second, pull_in_second = jax.vjp(rms_norm, first_f32, gains[1, 0])
    normed_second, down_second = spread_rows(normed_second.astype(BF16), stages, down_second)
    second, weights_second, kept_second, _, d_hidden_second = forward(
        first_f32,
        normed_second,
        mix_second,
        gate_up_second,
        gains[1],
        down_weight=down_second,
    )
    second_rows = jnp.stack([one_way(second, 0), second])
    d_first, (mix_1, gate_up_1, down_1), small_second, second_rows = backward(
        own_cotangent,
        d_down_second,
        d_hidden_second,
        weights_second,
        kept_second,
        pull_in_second,
        second_rows,
    )
    d_dealt, (mix_0, gate_up_begun, down_0), small_first, mix_1 = backward(
        d_first.astype(BF16).astype(F32), None, None, weights_first, kept_first, pull_in_first, mix_1
    )

    across = rep_stages[0]
    small = jnp.concatenate([small_first, small_second])
    for stage in shard_stages:
        small = small + swap(small, stage)
    d_dealt, mix_0, gate_up_diagonal, back_places, small = lax.optimization_barrier(
        (d_dealt, mix_0, swap(gate_up_begun[1], across), back_places, small)
    )
    mix_own, mix_other, mix_across = begin_collect(mix_0, mix_1)
    rows_sent = [d_dealt, small, jnp.zeros((8, model_width), F32)]
    grads = spread(jnp.concatenate(rows_sent).astype(BF16)[None], rep_stages[:1])
    gate, up = place_columns(collect(*gate_up_begun, gate_up_diagonal), ident, shards)
    down_0, mix_other, mix_across, grads, gate, up = lax.optimization_barrier(
        (down_0, mix_other, mix_across, grads, gate, up)
    )
    down_own, down_other, down_across = begin_collect(down_0, down_1)
    mix_diagonal = swap(mix_other, across)
    down_other, down_across, mix_diagonal, grads = lax.optimization_barrier(
        (down_other, down_across, mix_diagonal, spread(grads, stages[:1]))
    )
    down_diagonal = swap(down_other, across)
    grads = spread(grads, rep_stages[1:-1])
    far_grads = swap(grads, stages[-1])
    sources = [ident ^ code for code in range(group)]
    columns = jnp.stack(
        [head_number(device, t) * head for device in sources for t in range(per_device)]
    )
    corners = []
    for device in sources:
        corners += [device // sharing * each * head, device % sharing * (model_width // sharing)]
    small = jnp.sum(grads[:, length:].astype(F32), axis=0)
    small = (small + jnp.sum(far_grads[:, length:].astype(F32), axis=0))[:8]
    small = lax.dynamic_slice(
        small, (4 * section, shard * local_rows), (4, local_rows)
    )

    near_count = grads.shape[0]
    back_rows = []
    for number in range(micro):
        place = back_places[number]
        start = (place % near_count, 0, 0)
        near, far = [
            lax.dynamic_slice(value, start, (1, length, model_width))
            for value in (grads, far_grads)
        ]
        back_rows.append(jnp.where(place < near_count, near, far))
    boundary_out = jnp.where(on_first, jnp.concatenate(back_rows), second_rows).reshape(
        1, micro * length, model_width
    )
    down_diagonal, boundary_out, small = lax.optimization_barrier(
        (down_diagonal, boundary_out, small)
    )
    query, forget, into, out = place_mixer(
        collect(mix_own, mix_other, mix_across, mix_diagonal),
        columns,
        jnp.stack(corners),
        each * head,
        model_width,
    )
    down = place_rows(collect(down_own, down_other, down_across, down_diagonal), ident)

    return (
        boundary_out,
        query[None],
        forget[None],
        into[None],
        out[None],
        gate[None],
        up[None],
        down[None],
        small[0][None],
        small[2][None],
        small[1][None],
        small[3][None],
    )


def solution(mesh):
    row_blocks = P("section", ("shard", "rep"), None)
    weight = P("section", "shard", None)
    vector = P("section", "shard")
    return jax.shard_map(
        local,
        mesh=mesh,
        in_specs=(row_blocks, P(("shard", "rep"), None), P(("shard", "rep")))
        + (weight,) * 7
        + (vector,) * 4,
        out_specs=(row_blocks,) + (weight,) * 7 + (vector,) * 4,
        check_vma=False,
    )
```
